512 devices in a mesh: rep: 16 (over z, core), fsdp: 32 (over y, x).
Axes of the slice: x: 4, y: 8, z: 8, core: 2. Of those that a mesh axis runs over, the one named last changes fastest.
Arguments:
- activations: bfloat16 [131072, 6144], P(('rep', 'fsdp')), may hold values from -6 to 6
- unit_grads: bfloat16 [131072, 128], P(('rep', 'fsdp')), may hold values from -0.0625 to 0.0625
- momentum: float32 [16, 6144, 128], P('rep', 'fsdp'), may hold values from -6 to 6
- weights: float32 [6144, 128], P('fsdp'), may hold values from -0.75 to 0.75
- block_ids: int32 [16, 192, 6], P('rep', 'fsdp'), may hold values from 0 to 31, as said below
- block_counts: int32 [16, 192], P('rep', 'fsdp'), may hold values from 1 to 6, as said below
Outputs:
- new_weights: float32 [6144, 128], P('fsdp')
- new_momentum: float32 [16, 6144, 128], P('rep', 'fsdp')
The draws below stay inside these ranges and needn't reach their ends.
Inputs may be any that keep to these rules, and one draw needn't show every extreme that they name: `block_counts`: every replica has a tile with 6 live slots. `block_ids`: the live slots of a tile name different blocks; slots at or past the count hold 0.
All inputs are finite; a program needn't handle non-finite values.
Results may differ from the reference program's by a relative error of at most 0.0055.
Values may be sent and summed in bfloat16 or wider, within the bound.
A program may use at most 64 MiB of HBM per device.

```python
import jax
import jax.numpy as jnp
from jax import lax

D = 6144
EDGE = 64
NBLK = 32
SLOTS = 6
FW = 128
TILES = 192
TOKR = 8192
TOKENS = 131072
N_REP = 16


def shared_lists(key):
    count_key, heavy_key, place_key, order_key = jax.random.split(key, 4)
    light = jax.random.randint(count_key, (N_REP, TILES), 1, 3)
    heavy = jax.random.randint(heavy_key, (N_REP, TILES), 0, 16) == 0
    place = jax.random.randint(place_key, (N_REP, 1), 0, TILES)
    forced = jnp.arange(TILES, dtype=jnp.int32)[None, :] == place
    counts = jnp.where(heavy | forced, SLOTS, light).astype(jnp.int32)
    scores = jax.random.randint(order_key, (N_REP, TILES, NBLK), 0, 1 << 20) * NBLK + jnp.arange(NBLK, dtype=jnp.int32)
    order = jnp.argsort(scores, axis=-1)[:, :, :SLOTS].astype(jnp.int32)
    active = jnp.arange(SLOTS, dtype=jnp.int32)[None, None, :] < counts[:, :, None]
    chosen = jnp.where(active, order, 0).astype(jnp.int32)
    return (chosen, counts)


def draw_block_ids(key, part):
    return shared_lists(key)[0]


def draw_block_counts(key, part):
    return shared_lists(key)[1]


def shard_levels(rng, dims, cuts, low, top_value):
    factor_of, own = 1.0, jax.random.fold_in(rng, 6)
    for position, shards_of in cuts:
        steps = jnp.exp(jax.random.uniform(jax.random.fold_in(own, position), (shards_of,), jnp.float32, low / len(cuts), top_value / len(cuts)))
        factor_of = factor_of * jnp.repeat(steps, dims[position] // shards_of).reshape([-1 if axis == position else 1 for axis in range(len(dims))])
    return factor_of


def centred(rng, dims, deviation, reach, shards=(), kind=jnp.bfloat16):
    loudness = shard_levels(rng, dims, shards, -0.22, 0.18) if shards else 1.0
    values = jax.random.normal(rng, dims, jnp.float32) * deviation * loudness
    return jnp.minimum(jnp.maximum(values, -reach), reach).astype(kind)


def setup_inputs(seed: int = 0) -> dict:
    seeds = jax.random.split(jax.random.key(seed), 7)
    return {
        "activations": centred(seeds[0], (TOKENS, D), 1.0, 6.0, ((0, 512),)),
        "unit_grads": centred(seeds[1], (TOKENS, FW), TOKR ** -0.5, 0.0625, ((0, 512),)),
        "momentum": centred(seeds[2], (N_REP, D, FW), 1.0, 6.0, ((0, 16), (1, 32)), jnp.float32),
        "weights": centred(seeds[3], (D, FW), 0.05, 0.75, ((0, 32),), jnp.float32),
        "block_ids": draw_block_ids(jax.random.fold_in(seeds[6], 71), 0),
        "block_counts": draw_block_counts(jax.random.fold_in(seeds[6], 71), 0),
    }


def cosine_table(edge):
    freq = jnp.arange(edge, dtype=jnp.float32)[:, None]
    place = jnp.arange(edge, dtype=jnp.float32)[None, :]
    factor = jnp.where(freq == 0, jnp.sqrt(1.0 / edge), jnp.sqrt(2.0 / edge))
    return factor * jnp.cos(jnp.pi * (2.0 * place + 1.0) * freq / (2.0 * edge))

def forward_tiles(moment4, table):
    partial_rows = jnp.einsum('ui,aibj->aubj', table, moment4, precision=lax.Precision.HIGHEST)
    return jnp.einsum('aubj,vj->abuv', partial_rows, table, precision=lax.Precision.HIGHEST)

def inverse_tiles(coeffs4, table):
    partial_rows = jnp.einsum('ui,abuv->aibv', table, coeffs4, precision=lax.Precision.HIGHEST)
    return jnp.einsum('aibv,vj->aibj', partial_rows, table, precision=lax.Precision.HIGHEST)

def reference(activations, unit_grads, momentum, weights, block_ids, block_counts):
    table = cosine_table(EDGE)
    rows_a = D // EDGE
    cols_b = FW // EDGE
    inputs = activations.reshape(N_REP, TOKR, D)
    grads = unit_grads.reshape(N_REP, TOKR, FW)

    def per_replica(items):
        inp, ugr, mom_old, chosen, counts = items
        gradient = lax.dot_general(inp, ugr, (((0,), (0,)), ((), ())), preferred_element_type=jnp.float32)
        moment = 0.9 * mom_old + gradient
        coeffs = forward_tiles(moment.reshape(rows_a, EDGE, cols_b, EDGE), table).reshape(TILES, NBLK, 128)
        active = (jnp.arange(SLOTS, dtype=jnp.int32)[None, :] < counts[:, None]).astype(jnp.float32)
        onehot = (chosen[:, :, None] == jnp.arange(NBLK, dtype=jnp.int32)[None, None, :]).astype(jnp.float32)
        onehot = onehot * active[:, :, None]
        picked = jnp.einsum('tkn,tnc->tkc', onehot, coeffs, precision=lax.Precision.HIGHEST).astype(jnp.bfloat16)
        removed = jnp.einsum('tkn,tkc->tnc', onehot, picked.astype(jnp.float32), precision=lax.Precision.HIGHEST)
        taken = inverse_tiles(removed.reshape(rows_a, cols_b, EDGE, EDGE), table).reshape(D, FW)
        return (moment - taken, removed)
    new_momentum, removed_all = lax.map(per_replica, (inputs, grads, momentum, block_ids, block_counts))
    summed = lax.optimization_barrier(jnp.sum(removed_all, axis=0))
    update = inverse_tiles(summed.reshape(rows_a, cols_b, EDGE, EDGE), table)
    spread = jnp.sqrt(lax.optimization_barrier(jnp.mean(update * update, axis=(1, 3), keepdims=True)) + 1e-06)
    new_weights = weights - 0.25 * jnp.tanh(update / spread).reshape(D, FW)
    return (new_weights, new_momentum)
```

```python
import functools

import jax
import jax.numpy as jnp
import ml_dtypes
import numpy as np
from jax import lax
from jax.experimental import pallas as pl
from jax.experimental.pallas import tpu as pltpu
from jax.sharding import PartitionSpec as P

MESH = pl.DeviceIdType.MESH
F32 = jnp.float32
BF16 = jnp.bfloat16

EDGE = 64
NBLK = 32
SLOTS = 6
FW = 128
NX, NY, NREP = 4, 8, 16
TILE_ROWS = 3
ROWS = TILE_ROWS * EDGE
GROUP = NX * ROWS
TOK = 256
H1 = 64
H2 = ROWS - H1
ORDER = (4, 3, 5, 2, 6, 1, 7, 0)
STREAMS = 4


def tables():
    freq = np.arange(EDGE)[:, None].astype(np.float64)
    place = np.arange(EDGE)[None, :].astype(np.float64)
    factor = np.where(freq == 0, np.sqrt(1.0 / EDGE), np.sqrt(2.0 / EDGE))
    table = (factor * np.cos(np.pi * (2.0 * place + 1.0) * freq / (2.0 * EDGE))).astype(np.float32)

    def halves(m):
        hi = m.astype(ml_dtypes.bfloat16)
        lo = (m - hi.astype(np.float32)).astype(ml_dtypes.bfloat16)
        return hi, lo

    both = np.zeros((2 * EDGE, 2 * EDGE), np.float32)
    both[:EDGE, :EDGE] = table
    both[EDGE:, EDGE:] = table
    split = np.concatenate([table[0::2], table[1::2]], axis=0)
    hi, lo = halves(both.T)
    right_fwd = np.concatenate([hi, hi, lo], axis=0)
    hi, lo = halves(both)
    right_inv = np.concatenate([hi, lo, hi], axis=0)
    hi, lo = halves(split)
    left_fwd = np.concatenate([hi, hi, lo], axis=1)
    hi, lo = halves(split.T)
    left_inv = np.concatenate([hi, hi, lo], axis=1)
    return right_fwd, right_inv, left_fwd, left_inv


def dot(a, b):
    return jnp.dot(a, b, preferred_element_type=F32)


def parts_of(v):
    hi = v.astype(BF16)
    lo = (v - hi.astype(F32)).astype(BF16)
    return hi, lo


def kernel(
    a_hbm, u_hbm, mom_hbm, w_hbm, ids_ref, cnt_ref, rf_hbm, ri_hbm, lf_hbm, li_hbm,
    nw_ref, nm_ref,
    a_vm, u_vm, mom_vm, w_vm, rf_vm, ri_vm, lf_vm, li_vm,
    part, y_slots, x_slots, r1, r2, x1_slots, y2_slots,
    code, codes, spread_w, listed, stage, moment_vm,
    load_sem, in_sem,
    y_send, y_recv, x_send, x_recv, x1_send, x1_recv, y2_send, y2_recv,
    c_send, c_recv, g_send, g_recv,
):
    rep = lax.axis_index("rep")
    pos = lax.axis_index("fsdp")
    y = pos // NX
    x = pos % NX

    def at_y(off):
        return ((y + off) % NY) * NX + x

    def at_x(off):
        return y * NX + (x + off) % NX

    def at_rep(off):
        return (rep + off) % NREP

    def load(j):
        t = (y + ORDER[j]) % NY
        cols = pl.ds(pl.multiple_of(t * GROUP, GROUP), GROUP)
        return pltpu.make_async_copy(a_hbm.at[:, cols], a_vm.at[j], load_sem.at[j])

    u_copy = pltpu.make_async_copy(u_hbm, u_vm, in_sem.at[0])
    u_copy.start()
    for j in range(NY):
        load(j).start()
    others = [
        pltpu.make_async_copy(src, dst, in_sem.at[n + 1])
        for n, (src, dst) in enumerate(
            [(mom_hbm, mom_vm), (w_hbm, w_vm), (rf_hbm, rf_vm), (ri_hbm, ri_vm), (lf_hbm, lf_vm), (li_hbm, li_vm)]
        )
    ]
    for copy in others:
        copy.start()

    barrier = pltpu.get_barrier_semaphore()
    for off in range(1, NY):
        pl.semaphore_signal(barrier, inc=1, device_id=(rep, at_y(off)), device_id_type=MESH)
    for off in range(1, NX):
        pl.semaphore_signal(barrier, inc=1, device_id=(rep, at_x(off)), device_id_type=MESH)
    for off in range(1, NREP):
        pl.semaphore_signal(barrier, inc=1, device_id=(at_rep(off), pos), device_id_type=MESH)

    lane8 = lax.broadcasted_iota(jnp.int32, (8, 128), 1)
    row8 = lax.broadcasted_iota(jnp.int32, (8, 128), 0)
    own = lane8 - (rep % 8) * 16
    target = [
        [jnp.where(k < cnt_ref[0, t], ids_ref[0, t, k], -64) for k in range(SLOTS)] for t in range(2 * TILE_ROWS)
    ]
    codes_own = jnp.where((own >= 0) & (own < 16), -64, 0)
    for k in range(SLOTS):
        column = jnp.zeros((8, 128), jnp.int32)
        for t in range(2 * TILE_ROWS):
            column = jnp.where(row8 == t, target[t][k], column)
        codes_own = jnp.where(own == k, column, codes_own)
        codes_own = jnp.where(own == k + SLOTS, column + NBLK, codes_own)
    code[...] = codes_own
    codes[rep] = codes_own

    def remote(src, dst, send, recv, device):
        return pltpu.make_async_remote_copy(
            src_ref=src, dst_ref=dst, send_sem=send, recv_sem=recv, device_id=device, device_id_type=MESH
        )

    y_streams = ((0, 1, 4, 0), (2, -1, 4, 4), (2, 1, 3, 8), (0, -1, 3, 11))

    def y_copy(stream, step):
        xs, way, length, first = y_streams[stream]
        n = first + step
        if step == 0:
            j = ORDER.index((way * length) % NY)
            src = part.at[j, pl.ds(xs, 2), pl.ds(0, H1)]
        else:
            src = y_slots.at[n - 1]
        return remote(src, y_slots.at[n], y_send.at[n], y_recv.at[n], (rep, at_y(way)))

    def y_add(stream, step):
        xs, way, length, first = y_streams[stream]
        y_copy(stream, step).wait_recv()
        j = ORDER.index((way * (length - 1 - step)) % NY)
        n = first + step
        y_slots[n] = (y_slots[n].astype(F32) + part[j, xs : xs + 2, 0:H1].astype(F32)).astype(BF16)

    def x_way(q):
        return 1 if q % 2 == 0 else -1

    def x_copy(q, which):
        way = x_way(q)
        n = 3 * q + which
        rows = pl.ds(2 * q, 2)
        if which == 0:
            src = part.at[rows, (x + 2) % NX, pl.ds(H1, H2)]
        elif which == 1:
            src = x_slots.at[3 * q]
        else:
            src = part.at[rows, (x - way) % NX, pl.ds(H1, H2)]
            way = -way
        return remote(src, x_slots.at[n], x_send.at[n], x_recv.at[n], (rep, at_x(way)))

    def x_mid(q):
        x_copy(q, 0).wait_recv()
        mine = part[2 * q : 2 * q + 2, (x + x_way(q)) % NX, H1:ROWS]
        x_slots[3 * q] = (x_slots[3 * q].astype(F32) + mine.astype(F32)).astype(BF16)
        x_copy(q, 1).start()

    def y2_copy(off):
        j = ORDER.index(off)
        return remote(r2.at[j], y2_slots.at[off - 1], y2_send.at[off - 1], y2_recv.at[off - 1], (rep, at_y(off)))

    def x_last(q):
        x_copy(q, 2).wait_recv()
        x_copy(q, 1).wait_recv()
        mine = part[2 * q : 2 * q + 2, x, H1:ROWS].astype(F32)
        total = mine + x_slots[3 * q + 1].astype(F32) + x_slots[3 * q + 2].astype(F32)
        r2[2 * q : 2 * q + 2] = total.astype(BF16)
        for off in ORDER[2 * q : 2 * q + 2]:
            if off:
                y2_copy(off).start()

    def x1_copy(off):
        return remote(
            r1.at[(x + off) % NX], x1_slots.at[off - 1], x1_send.at[off - 1], x1_recv.at[off - 1], (rep, at_x(off))
        )

    def c_copy(off):
        return remote(code, codes.at[rep], c_send.at[off - 1], c_recv.at[off - 1], (at_rep(off), pos))

    def g_copy(off):
        mine = listed.at[:, rep]
        return remote(mine, mine, g_send.at[off - 1], g_recv.at[off - 1], (at_rep(off), pos))

    pl.semaphore_wait(barrier, NY - 1 + NX - 1 + NREP - 1)
    u_copy.wait()

    for j in range(NY):
        load(j).wait()
        rows = lax.dot_general(a_vm[j], u_vm[...], (((0,), (0,)), ((), ())), preferred_element_type=F32)
        part[j] = rows.astype(BF16).reshape(NX, ROWS, FW)
        if j == 0:
            y_copy(0, 0).start()
            y_copy(1, 0).start()
        if j == 1:
            y_copy(2, 0).start()
        if j == 2:
            y_copy(3, 0).start()
        if j % 2 == 1:
            x_copy(j // 2, 0).start()
            x_copy(j // 2, 2).start()

    for off in range(1, NREP):
        c_copy(off).start()

    def y_round(step):
        for stream in range(4):
            if step < y_streams[stream][2] - 1:
                y_add(stream, step)
                y_copy(stream, step + 1).start()

    y_round(0)
    x_mid(0)
    x_mid(1)
    y_round(1)
    x_mid(2)
    x_mid(3)
    x_last(0)
    x_last(1)
    y_round(2)
    x_last(2)
    x_last(3)

    for half in range(2):
        xs = 2 * half
        total = part[ORDER.index(0), xs : xs + 2, 0:H1].astype(F32)
        for stream in range(4):
            if y_streams[stream][0] == xs:
                last = y_streams[stream][2] - 1
                y_copy(stream, last).wait_recv()
                total += y_slots[y_streams[stream][3] + last].astype(F32)
        r1[xs : xs + 2] = total.astype(BF16)
    for off in range(1, NX):
        x1_copy(off).start()

    for off in range(1, NREP):
        c_copy(off).wait_recv()
    row64 = lax.broadcasted_iota(jnp.int32, (EDGE, 128), 0)
    lane64 = lax.broadcasted_iota(jnp.int32, (EDGE, 128), 1)
    for side in range(NREP // 8):
        tile = codes[8 * side]
        for r in range(1, 8):
            tile += codes[8 * side + r]
        for t in range(2 * TILE_ROWS):
            hit = (tile[t : t + 1] == row64).astype(F32).astype(BF16)
            spread_w[t // 2, EDGE * (t % 2) : EDGE * (t % 2) + EDGE, 128 * side : 128 * side + 128] = hit

    for copy in others:
        copy.wait()

    g1 = r1[x].astype(F32)
    for off in range(1, NX):
        x1_copy(off).wait_recv()
        g1 += x1_slots[off - 1].astype(F32)
    moment_vm[0:H1] = 0.9 * mom_vm[0, 0:H1] + g1
    g2 = r2[ORDER.index(0)].astype(F32)
    for off in range(1, NY):
        y2_copy(off).wait_recv()
        g2 += y2_slots[off - 1].astype(F32)
    moment_vm[H1:ROWS] = 0.9 * mom_vm[0, H1:ROWS] + g2
    moment = moment_vm[...]

    def left(table, v):
        out = []
        for a in range(TILE_ROWS):
            hi, lo = parts_of(v[a * EDGE : a * EDGE + EDGE])
            out.append(dot(table, jnp.concatenate([hi, lo, hi], axis=0)))
        return jnp.concatenate(out, axis=0)

    hi, lo = parts_of(moment)
    coeffs = left(lf_vm[...], dot(jnp.concatenate([hi, lo, hi], axis=1), rf_vm[...])).astype(BF16).astype(F32)
    low_lanes = lane64 < EDGE
    block64 = row64 % NBLK
    keep = []
    stage[...] = jnp.zeros_like(stage)
    for a in range(TILE_ROWS):
        tile = coeffs[a * EDGE : a * EDGE + EDGE]
        live = jnp.zeros((EDGE, 128), F32)
        for k in range(SLOTS):
            chosen = jnp.where(low_lanes, target[2 * a][k], target[2 * a + 1][k]) == block64
            live = jnp.where(chosen, 1.0, live)
            rows = jnp.where(chosen, tile, 0.0)
            stage[a, k : k + 1] = jnp.sum(rows[0:NBLK], axis=0, keepdims=True)
            stage[a, SLOTS + k : SLOTS + k + 1] = jnp.sum(rows[NBLK:EDGE], axis=0, keepdims=True)
        keep.append(tile * live)
    listed[:, rep] = stage[...].astype(BF16)
    for off in range(1, NREP):
        g_copy(off).start()

    removed = jnp.concatenate(keep, axis=0).astype(BF16)
    right_inv = ri_vm[...]
    taken = left(li_vm[...], dot(jnp.concatenate([removed, removed], axis=1), right_inv[0:256]))
    nm_ref[0] = moment - taken

    for off in range(1, NREP):
        g_copy(off).wait_recv()

    summed = []
    for a in range(TILE_ROWS):
        rows = dot(spread_w[a], listed[a].reshape(NREP * 16, 128))
        summed.append(jnp.where(low_lanes, rows[0:EDGE], rows[EDGE : 2 * EDGE]))
    hi, lo = parts_of(jnp.concatenate(summed, axis=0))
    update = left(li_vm[...], dot(jnp.concatenate([hi, hi, lo], axis=1), right_inv))
    lane1 = lax.broadcasted_iota(jnp.int32, (1, 128), 1) < EDGE
    for a in range(TILE_ROWS):
        tile = update[a * EDGE : a * EDGE + EDGE]
        squares = jnp.sum(tile * tile, axis=0, keepdims=True)
        first = jnp.sum(jnp.where(lane1, squares, 0.0), axis=1, keepdims=True)
        second = jnp.sum(jnp.where(lane1, 0.0, squares), axis=1, keepdims=True)
        scale = lax.rsqrt(jnp.where(lane1, first, second) * (1.0 / (EDGE * EDGE)) + 1e-6)
        span = slice(a * EDGE, a * EDGE + EDGE)
        nw_ref[span] = w_vm[span] - 0.25 * jnp.tanh(tile * scale)

    for stream in range(4):
        for step in range(y_streams[stream][2]):
            y_copy(stream, step).wait_send()
    for q in range(STREAMS):
        for which in range(3):
            x_copy(q, which).wait_send()
    for off in range(1, NX):
        x1_copy(off).wait_send()
    for off in range(1, NY):
        y2_copy(off).wait_send()
    for off in range(1, NREP):
        c_copy(off).wait_send()
        g_copy(off).wait_send()


def on_device(activations, unit_grads, momentum, weights, block_ids, block_counts):
    right_fwd, right_inv, left_fwd, left_inv = tables()
    any_spec = pl.BlockSpec(memory_space=pl.ANY)
    smem = pl.BlockSpec(memory_space=pltpu.SMEM)
    vmem = pl.BlockSpec(memory_space=pltpu.VMEM)
    dma = pltpu.SemaphoreType.DMA
    new_weights, new_momentum = pl.pallas_call(
        kernel,
        out_shape=(
            jax.ShapeDtypeStruct(weights.shape, F32),
            jax.ShapeDtypeStruct(momentum.shape, F32),
        ),
        in_specs=[any_spec] * 4 + [smem] * 2 + [any_spec] * 4,
        out_specs=(vmem, vmem),
        scratch_shapes=[
            pltpu.VMEM((NY, TOK, GROUP), BF16),
            pltpu.VMEM((TOK, FW), BF16),
            pltpu.VMEM((1, ROWS, FW), F32),
            pltpu.VMEM((ROWS, FW), F32),
            pltpu.VMEM(right_fwd.shape, BF16),
            pltpu.VMEM(right_inv.shape, BF16),
            pltpu.VMEM(left_fwd.shape, BF16),
            pltpu.VMEM(left_inv.shape, BF16),
            pltpu.VMEM((NY, NX, ROWS, FW), BF16),
            pltpu.VMEM((14, 2, H1, FW), BF16),
            pltpu.VMEM((3 * STREAMS, 2, H2, FW), BF16),
            pltpu.VMEM((NX, H1, FW), BF16),
            pltpu.VMEM((NY, H2, FW), BF16),
            pltpu.VMEM((NX - 1, H1, FW), BF16),
            pltpu.VMEM((NY - 1, H2, FW), BF16),
            pltpu.VMEM((8, 128), jnp.int32),
            pltpu.VMEM((NREP, 8, 128), jnp.int32),
            pltpu.VMEM((TILE_ROWS, 2 * EDGE, NREP * 16), BF16),
            pltpu.VMEM((TILE_ROWS, NREP, 16, 128), BF16),
            pltpu.VMEM((TILE_ROWS, 16, 128), F32),
            pltpu.VMEM((ROWS, FW), F32),
            dma((NY,)),
            dma((7,)),
            dma((14,)), dma((14,)),
            dma((3 * STREAMS,)), dma((3 * STREAMS,)),
            dma((NX - 1,)), dma((NX - 1,)),
            dma((NY - 1,)), dma((NY - 1,)),
            dma((NREP - 1,)), dma((NREP - 1,)),
            dma((NREP - 1,)), dma((NREP - 1,)),
        ],
        compiler_params=pltpu.CompilerParams(
            collective_id=0, has_side_effects=True, vmem_limit_bytes=40 * 1024 * 1024
        ),
    )(activations, unit_grads, momentum, weights, block_ids, block_counts, right_fwd, right_inv, left_fwd, left_inv)
    return new_weights, new_momentum


def solution(mesh):
    placed = (
        P(("rep", "fsdp"), None),
        P(("rep", "fsdp"), None),
        P("rep", "fsdp", None),
        P("fsdp", None),
        P("rep", "fsdp", None),
        P("rep", "fsdp"),
    )
    return jax.shard_map(
        on_device,
        mesh=mesh,
        in_specs=placed,
        out_specs=(P("fsdp", None), P("rep", "fsdp", None)),
        check_vma=False,
    )
```

```python
import functools

import jax
import jax.numpy as jnp
import ml_dtypes
import numpy as np
from jax import lax
from jax.experimental import pallas as pl
from jax.experimental.pallas import tpu as pltpu
from jax.sharding import PartitionSpec as P

MESH = pl.DeviceIdType.MESH
F32 = jnp.float32
BF16 = jnp.bfloat16

EDGE = 64
NBLK = 32
SLOTS = 6
FW = 128
NX, NY, NREP = 4, 8, 16
TILE_ROWS = 3
ROWS = TILE_ROWS * EDGE
GROUP = NX * ROWS
TOK = 256
H1 = 96
H2 = ROWS - H1
ORDER = (4, 3, 5, 2, 6, 1, 7, 0)
STREAMS = 4


def tables():
    freq = np.arange(EDGE)[:, None].astype(np.float64)
    place = np.arange(EDGE)[None, :].astype(np.float64)
    factor = np.where(freq == 0, np.sqrt(1.0 / EDGE), np.sqrt(2.0 / EDGE))
    table = (factor * np.cos(np.pi * (2.0 * place + 1.0) * freq / (2.0 * EDGE))).astype(np.float32)

    def halves(m):
        hi = m.astype(ml_dtypes.bfloat16)
        lo = (m - hi.astype(np.float32)).astype(ml_dtypes.bfloat16)
        return hi, lo

    both = np.zeros((2 * EDGE, 2 * EDGE), np.float32)
    both[:EDGE, :EDGE] = table
    both[EDGE:, EDGE:] = table
    split = np.concatenate([table[0::2], table[1::2]], axis=0)
    hi, lo = halves(both.T)
    right_fwd = np.concatenate([hi, hi, lo], axis=0)
    hi, lo = halves(both)
    right_inv = np.concatenate([hi, lo, hi], axis=0)
    hi, lo = halves(split)
    left_fwd = np.concatenate([hi, hi, lo], axis=1)
    hi, lo = halves(split.T)
    left_inv = np.concatenate([hi, hi, lo], axis=1)
    return right_fwd, right_inv, left_fwd, left_inv


def dot(a, b):
    return jnp.dot(a, b, preferred_element_type=F32)


def parts_of(v):
    hi = v.astype(BF16)
    lo = (v - hi.astype(F32)).astype(BF16)
    return hi, lo


def kernel(
    a_hbm, u_hbm, mom_hbm, w_hbm, ids_hbm, cnt_hbm, rf_hbm, ri_hbm, lf_hbm, li_hbm,
    nw_ref, nm_ref,
    a_vm, u_vm, mom_vm, w_vm, rf_vm, ri_vm, lf_vm, li_vm,
    ids_ref, cnt_ref, part, y_slots, x_slots, r1, r2, x1_slots, y2_slots,
    code, codes, spread_w, listed, stage, moment_vm,
    load_sem, in_sem,
    y_send, y_recv, x_send, x_recv, x1_send, x1_recv, y2_send, y2_recv,
    c_send, c_recv, g_send, g_recv,
):
    rep = lax.axis_index("rep")
    pos = lax.axis_index("fsdp")
    y = pos // NX
    x = pos % NX

    def at_y(off):
        return ((y + off) % NY) * NX + x

    def at_x(off):
        return y * NX + (x + off) % NX

    def at_rep(off):
        return (rep + off) % NREP

    def load(j):
        t = (y + ORDER[j]) % NY
        cols = pl.ds(pl.multiple_of(t * GROUP, GROUP), GROUP)
        return pltpu.make_async_copy(a_hbm.at[:, cols], a_vm.at[j], load_sem.at[j])

    u_copy = pltpu.make_async_copy(u_hbm, u_vm, in_sem.at[0])
    others = [
        pltpu.make_async_copy(src, dst, in_sem.at[n + 1])
        for n, (src, dst) in enumerate(
            [(ids_hbm, ids_ref), (cnt_hbm, cnt_ref), (mom_hbm, mom_vm), (w_hbm, w_vm), (rf_hbm, rf_vm), (ri_hbm, ri_vm), (lf_hbm, lf_vm), (li_hbm, li_vm)]
        )
    ]
    for copy in others[0:2]:
        copy.start()
    u_copy.start()
    for j in range(NY):
        load(j).start()
    for copy in others[2:]:
        copy.start()

    barrier = pltpu.get_barrier_semaphore()
    for off in range(1, NY):
        pl.semaphore_signal(barrier, inc=1, device_id=(rep, at_y(off)), device_id_type=MESH)
    for off in range(1, NX):
        pl.semaphore_signal(barrier, inc=1, device_id=(rep, at_x(off)), device_id_type=MESH)
    for off in range(1, NREP):
        pl.semaphore_signal(barrier, inc=1, device_id=(at_rep(off), pos), device_id_type=MESH)

    for copy in others[0:2]:
        copy.wait()
    lane8 = lax.broadcasted_iota(jnp.int32, (8, 128), 1)
    row8 = lax.broadcasted_iota(jnp.int32, (8, 128), 0)
    own = lane8 - (rep % 8) * 16
    target = [
        [jnp.where(k < cnt_ref[0, t], ids_ref[t, 0, k], -64) for k in range(SLOTS)] for t in range(2 * TILE_ROWS)
    ]
    codes_own = jnp.where((own >= 0) & (own < 16), -64, 0)
    for k in range(SLOTS):
        column = jnp.zeros((8, 128), jnp.int32)
        for t in range(2 * TILE_ROWS):
            column = jnp.where(row8 == t, target[t][k], column)
        codes_own = jnp.where(own == k, column, codes_own)
        codes_own = jnp.where(own == k + SLOTS, column + NBLK, codes_own)
    code[...] = codes_own
    codes[rep] = codes_own

    started = []

    class Sent:
        def __init__(self, src, dst, send, recv, device):
            self.copy = pltpu.make_async_remote_copy(
                src_ref=src, dst_ref=dst, send_sem=send, recv_sem=recv, device_id=device, device_id_type=MESH
            )

        def start(self):
            self.copy.start()
            started.append(self.copy)

        def wait_recv(self):
            self.copy.wait_recv()

    remote = Sent

    y_streams = ((0, 1, 4, 0), (2, -1, 4, 4), (2, 1, 3, 8), (0, -1, 3, 11))

    def y_copy(stream, step):
        xs, way, length, first = y_streams[stream]
        n = first + step
        if step == 0:
            j = ORDER.index((way * length) % NY)
            src = part.at[j, pl.ds(xs, 2), pl.ds(0, H1)]
        else:
            src = y_slots.at[n - 1]
        return remote(src, y_slots.at[n], y_send.at[n], y_recv.at[n], (rep, at_y(way)))

    def y_add(stream, step):
        xs, way, length, first = y_streams[stream]
        y_copy(stream, step).wait_recv()
        j = ORDER.index((way * (length - 1 - step)) % NY)
        n = first + step
        y_slots[n] = (y_slots[n].astype(F32) + part[j, xs : xs + 2, 0:H1].astype(F32)).astype(BF16)

    def x_way(q):
        return 1 if q % 2 == 0 else -1

    def x_copy(q, which):
        way = x_way(q)
        n = 3 * q + which
        rows = pl.ds(2 * q, 2)
        if which == 0:
            src = part.at[rows, (x + 2) % NX, pl.ds(H1, H2)]
        elif which == 1:
            src = x_slots.at[3 * q]
        else:
            src = part.at[rows, (x - way) % NX, pl.ds(H1, H2)]
            way = -way
        return remote(src, x_slots.at[n], x_send.at[n], x_recv.at[n], (rep, at_x(way)))

    def x_mid(q):
        x_copy(q, 0).wait_recv()
        mine = part[2 * q : 2 * q + 2, (x + x_way(q)) % NX, H1:ROWS]
        x_slots[3 * q] = (x_slots[3 * q].astype(F32) + mine.astype(F32)).astype(BF16)
        x_copy(q, 1).start()

    def y2_copy(off):
        j = ORDER.index(off)
        return remote(r2.at[j], y2_slots.at[off - 1], y2_send.at[off - 1], y2_recv.at[off - 1], (rep, at_y(off)))

    def x_last(q):
        x_copy(q, 2).wait_recv()
        x_copy(q, 1).wait_recv()
        mine = part[2 * q : 2 * q + 2, x, H1:ROWS].astype(F32)
        total = mine + x_slots[3 * q + 1].astype(F32) + x_slots[3 * q + 2].astype(F32)
        r2[2 * q : 2 * q + 2] = total.astype(BF16)
        for off in ORDER[2 * q : 2 * q + 2]:
            if off:
                y2_copy(off).start()

    def x1_copy(off):
        return remote(
            r1.at[(x + off) % NX], x1_slots.at[off - 1], x1_send.at[off - 1], x1_recv.at[off - 1], (rep, at_x(off))
        )

    def c_copy(off):
        return remote(code, codes.at[rep], c_send.at[off - 1], c_recv.at[off - 1], (at_rep(off), pos))

    def g_copy(off):
        mine = listed.at[:, rep]
        return remote(mine, mine, g_send.at[off - 1], g_recv.at[off - 1], (at_rep(off), pos))

    pl.semaphore_wait(barrier, NY - 1 + NX - 1 + NREP - 1)
    u_copy.wait()

    for j in range(NY):
        load(j).wait()
        rows = lax.dot_general(a_vm[j], u_vm[...], (((0,), (0,)), ((), ())), preferred_element_type=F32)
        part[j] = rows.astype(BF16).reshape(NX, ROWS, FW)
        if j == 0:
            y_copy(0, 0).start()
            y_copy(1, 0).start()
        if j == 1:
            y_copy(2, 0).start()
        if j == 2:
            y_copy(3, 0).start()
        if j % 2 == 1:
            x_copy(j // 2, 0).start()
            x_copy(j // 2, 2).start()

    for off in range(1, NREP):
        c_copy(off).start()

    def y_round(step):
        for stream in range(4):
            if step < y_streams[stream][2] - 1:
                y_add(stream, step)
                y_copy(stream, step + 1).start()

    y_round(0)
    x_mid(0)
    x_mid(1)
    y_round(1)
    x_mid(2)
    x_mid(3)
    x_last(0)
    x_last(1)
    y_round(2)
    x_last(2)
    x_last(3)

    for half in range(2):
        xs = 2 * half
        total = part[ORDER.index(0), xs : xs + 2, 0:H1].astype(F32)
        for stream in range(4):
            if y_streams[stream][0] == xs:
                last = y_streams[stream][2] - 1
                y_copy(stream, last).wait_recv()
                total += y_slots[y_streams[stream][3] + last].astype(F32)
        r1[xs : xs + 2] = total.astype(BF16)
    for off in range(1, NX):
        x1_copy(off).start()

    for off in range(1, NREP):
        c_copy(off).wait_recv()
    row64 = lax.broadcasted_iota(jnp.int32, (EDGE, 128), 0)
    lane64 = lax.broadcasted_iota(jnp.int32, (EDGE, 128), 1)
    for side in range(NREP // 8):
        tile = codes[8 * side]
        for r in range(1, 8):
            tile += codes[8 * side + r]
        for t in range(2 * TILE_ROWS):
            hit = (tile[t : t + 1] == row64).astype(F32).astype(BF16)
            spread_w[t // 2, EDGE * (t % 2) : EDGE * (t % 2) + EDGE, 128 * side : 128 * side + 128] = hit

    for copy in others[2:]:
        copy.wait()

    g1 = r1[x].astype(F32)
    for off in range(1, NX):
        x1_copy(off).wait_recv()
        g1 += x1_slots[off - 1].astype(F32)
    moment_vm[0:H1] = 0.9 * mom_vm[0, 0:H1] + g1
    g2 = r2[ORDER.index(0)].astype(F32)
    for off in range(1, NY):
        y2_copy(off).wait_recv()
        g2 += y2_slots[off - 1].astype(F32)
    moment_vm[H1:ROWS] = 0.9 * mom_vm[0, H1:ROWS] + g2
    moment = moment_vm[...]

    def left(table, v):
        out = []
        for a in range(TILE_ROWS):
            hi, lo = parts_of(v[a * EDGE : a * EDGE + EDGE])
            out.append(dot(table, jnp.concatenate([hi, lo, hi], axis=0)))
        return jnp.concatenate(out, axis=0)

    hi, lo = parts_of(moment)
    coeffs = left(lf_vm[...], dot(jnp.concatenate([hi, lo, hi], axis=1), rf_vm[...])).astype(BF16).astype(F32)
    low_lanes = lane64 < EDGE
    block64 = row64 % NBLK
    keep = []
    stage[...] = jnp.zeros_like(stage)
    for a in range(TILE_ROWS):
        tile = coeffs[a * EDGE : a * EDGE + EDGE]
        live = jnp.zeros((EDGE, 128), F32)
        for k in range(SLOTS):
            chosen = jnp.where(low_lanes, target[2 * a][k], target[2 * a + 1][k]) == block64
            live = jnp.where(chosen, 1.0, live)
            rows = jnp.where(chosen, tile, 0.0)
            stage[a, k : k + 1] = jnp.sum(rows[0:NBLK], axis=0, keepdims=True)
            stage[a, SLOTS + k : SLOTS + k + 1] = jnp.sum(rows[NBLK:EDGE], axis=0, keepdims=True)
        keep.append(tile * live)
    listed[:, rep] = stage[...].astype(BF16)
    for off in range(1, NREP):
        g_copy(off).start()

    removed = jnp.concatenate(keep, axis=0).astype(BF16)
    right_inv = ri_vm[...]
    taken = left(li_vm[...], dot(jnp.concatenate([removed, removed], axis=1), right_inv[0:256]))
    nm_ref[0] = moment - taken

    for off in range(1, NREP):
        g_copy(off).wait_recv()

    summed = []
    for a in range(TILE_ROWS):
        rows = dot(spread_w[a], listed[a].reshape(NREP * 16, 128))
        summed.append(jnp.where(low_lanes, rows[0:EDGE], rows[EDGE : 2 * EDGE]))
    hi, lo = parts_of(jnp.concatenate(summed, axis=0))
    update = left(li_vm[...], dot(jnp.concatenate([hi, hi, lo], axis=1), right_inv))
    lane1 = lax.broadcasted_iota(jnp.int32, (1, 128), 1) < EDGE
    for a in range(TILE_ROWS):
        tile = update[a * EDGE : a * EDGE + EDGE]
        squares = jnp.sum(tile * tile, axis=0, keepdims=True)
        first = jnp.sum(jnp.where(lane1, squares, 0.0), axis=1, keepdims=True)
        second = jnp.sum(jnp.where(lane1, 0.0, squares), axis=1, keepdims=True)
        scale = lax.rsqrt(jnp.where(lane1, first, second) * (1.0 / (EDGE * EDGE)) + 1e-6)
        span = slice(a * EDGE, a * EDGE + EDGE)
        nw_ref[span] = w_vm[span] - 0.25 * jnp.tanh(tile * scale)

    for copy in started:
        copy.wait_send()


def on_device(activations, unit_grads, momentum, weights, block_ids, block_counts):
    right_fwd, right_inv, left_fwd, left_inv = tables()
    hbm = pl.BlockSpec(memory_space=pltpu.HBM)
    vmem = pl.BlockSpec(memory_space=pltpu.VMEM)
    dma = pltpu.SemaphoreType.DMA
    new_weights, new_momentum = pl.pallas_call(
        kernel,
        out_shape=(
            jax.ShapeDtypeStruct(weights.shape, F32),
            jax.ShapeDtypeStruct(momentum.shape, F32),
        ),
        in_specs=[hbm] * 10,
        out_specs=(vmem, vmem),
        scratch_shapes=[
            pltpu.VMEM((NY, TOK, GROUP), BF16),
            pltpu.VMEM((TOK, FW), BF16),
            pltpu.VMEM((1, ROWS, FW), F32),
            pltpu.VMEM((ROWS, FW), F32),
            pltpu.VMEM(right_fwd.shape, BF16),
            pltpu.VMEM(right_inv.shape, BF16),
            pltpu.VMEM(left_fwd.shape, BF16),
            pltpu.VMEM(left_inv.shape, BF16),
            pltpu.SMEM((2 * TILE_ROWS, 1, SLOTS), jnp.int32),
            pltpu.SMEM((1, 2 * TILE_ROWS), jnp.int32),
            pltpu.VMEM((NY, NX, ROWS, FW), BF16),
            pltpu.VMEM((14, 2, H1, FW), BF16),
            pltpu.VMEM((3 * STREAMS, 2, H2, FW), BF16),
            pltpu.VMEM((NX, H1, FW), BF16),
            pltpu.VMEM((NY, H2, FW), BF16),
            pltpu.VMEM((NX - 1, H1, FW), BF16),
            pltpu.VMEM((NY - 1, H2, FW), BF16),
            pltpu.VMEM((8, 128), jnp.int32),
            pltpu.VMEM((NREP, 8, 128), jnp.int32),
            pltpu.VMEM((TILE_ROWS, 2 * EDGE, NREP * 16), BF16),
            pltpu.VMEM((TILE_ROWS, NREP, 16, 128), BF16),
            pltpu.VMEM((TILE_ROWS, 16, 128), F32),
            pltpu.VMEM((ROWS, FW), F32),
            dma((NY,)),
            dma((9,)),
            dma((14,)), dma((14,)),
            dma((3 * STREAMS,)), dma((3 * STREAMS,)),
            dma((NX - 1,)), dma((NX - 1,)),
            dma((NY - 1,)), dma((NY - 1,)),
            dma((NREP - 1,)), dma((NREP - 1,)),
            dma((NREP - 1,)), dma((NREP - 1,)),
        ],
        compiler_params=pltpu.CompilerParams(
            collective_id=0, has_side_effects=True, vmem_limit_bytes=60 * 1024 * 1024
        ),
    )(activations, unit_grads, momentum, weights, jnp.transpose(block_ids, (1, 0, 2)), block_counts, right_fwd, right_inv, left_fwd, left_inv)
    return new_weights, new_momentum


def solution(mesh):
    placed = (
        P(("rep", "fsdp"), None),
        P(("rep", "fsdp"), None),
        P("rep", "fsdp", None),
        P("fsdp", None),
        P("rep", "fsdp", None),
        P("rep", "fsdp"),
    )
    return jax.shard_map(
        on_device,
        mesh=mesh,
        in_specs=placed,
        out_specs=(P("fsdp", None), P("rep", "fsdp", None)),
        check_vma=False,
    )
```

```python
import functools

import jax
import jax.numpy as jnp
import ml_dtypes
import numpy as np
from jax import lax
from jax.experimental import pallas as pl
from jax.experimental.pallas import tpu as pltpu
from jax.sharding import PartitionSpec as P

MESH = pl.DeviceIdType.MESH
F32 = jnp.float32
BF16 = jnp.bfloat16

EDGE = 64
NBLK = 32
SLOTS = 6
FW = 128
NX, NY, NREP = 4, 8, 16
TILE_ROWS = 3
ROWS = TILE_ROWS * EDGE
GROUP = NX * ROWS
TOK = 256
H1 = 64
H2 = ROWS - H1
ORDER = (4, 3, 5, 2, 6, 1, 7, 0)
STREAMS = 4


def tables():
    freq = np.arange(EDGE)[:, None].astype(np.float64)
    place = np.arange(EDGE)[None, :].astype(np.float64)
    factor = np.where(freq == 0, np.sqrt(1.0 / EDGE), np.sqrt(2.0 / EDGE))
    table = (factor * np.cos(np.pi * (2.0 * place + 1.0) * freq / (2.0 * EDGE))).astype(np.float32)

    def halves(m):
        hi = m.astype(ml_dtypes.bfloat16)
        lo = (m - hi.astype(np.float32)).astype(ml_dtypes.bfloat16)
        return hi, lo

    both = np.zeros((2 * EDGE, 2 * EDGE), np.float32)
    both[:EDGE, :EDGE] = table
    both[EDGE:, EDGE:] = table
    split = np.concatenate([table[0::2], table[1::2]], axis=0)
    hi, lo = halves(both.T)
    right_fwd = np.concatenate([hi, hi, lo], axis=0)
    hi, lo = halves(both)
    right_inv = np.concatenate([hi, lo, hi], axis=0)
    hi, lo = halves(split)
    left_fwd = np.concatenate([hi, hi, lo], axis=1)
    hi, lo = halves(split.T)
    left_inv = np.concatenate([hi, hi, lo], axis=1)
    return right_fwd, right_inv, left_fwd, left_inv


def dot(a, b):
    return jnp.dot(a, b, preferred_element_type=F32)


def parts_of(v):
    hi = v.astype(BF16)
    lo = (v - hi.astype(F32)).astype(BF16)
    return hi, lo


def kernel(
    a_hbm, u_hbm, mom_hbm, w_hbm, ids_hbm, cnt_hbm, rf_hbm, ri_hbm, lf_hbm, li_hbm,
    out_ref,
    a_vm, u_vm, mom_vm, w_vm, rf_vm, ri_vm, lf_vm, li_vm,
    ids_ref, cnt_ref, part, y_slots, x_slots, r1, r2, x1_slots, y2_slots,
    code, codes, spread_w, listed, stage, moment_vm,
    load_sem, in_sem,
    y_send, y_recv, x_send, x_recv, x1_send, x1_recv, y2_send, y2_recv,
    c_send, c_recv, g_send, g_recv,
):
    rep = lax.axis_index("rep")
    pos = lax.axis_index("fsdp")
    y = pos // NX
    x = pos % NX

    def at_y(off):
        return ((y + off) % NY) * NX + x

    def at_x(off):
        return y * NX + (x + off) % NX

    def at_rep(off):
        return (rep + off) % NREP

    def load(j):
        t = (y + ORDER[j]) % NY
        cols = pl.ds(pl.multiple_of(t * GROUP, GROUP), GROUP)
        return pltpu.make_async_copy(a_hbm.at[:, cols], a_vm.at[j], load_sem.at[j])

    u_copy = pltpu.make_async_copy(u_hbm, u_vm, in_sem.at[0])
    others = [
        pltpu.make_async_copy(src, dst, in_sem.at[n + 1])
        for n, (src, dst) in enumerate(
            [(ids_hbm, ids_ref), (cnt_hbm, cnt_ref), (mom_hbm, mom_vm), (w_hbm, w_vm), (rf_hbm, rf_vm), (ri_hbm, ri_vm), (lf_hbm, lf_vm), (li_hbm, li_vm)]
        )
    ]
    for copy in others[0:2]:
        copy.start()
    u_copy.start()
    for j in range(NY):
        load(j).start()
    for copy in others[2:]:
        copy.start()

    barrier = pltpu.get_barrier_semaphore()
    for off in range(1, NY):
        pl.semaphore_signal(barrier, inc=1, device_id=(rep, at_y(off)), device_id_type=MESH)
    for off in range(1, NX):
        pl.semaphore_signal(barrier, inc=1, device_id=(rep, at_x(off)), device_id_type=MESH)
    for off in range(1, NREP):
        pl.semaphore_signal(barrier, inc=1, device_id=(at_rep(off), pos), device_id_type=MESH)

    for copy in others[0:2]:
        copy.wait()
    lane8 = lax.broadcasted_iota(jnp.int32, (8, 128), 1)
    row8 = lax.broadcasted_iota(jnp.int32, (8, 128), 0)
    own = lane8 - (rep % 8) * 16
    target = [
        [jnp.where(k < cnt_ref[0, t], ids_ref[t, 0, k], -64) for k in range(SLOTS)] for t in range(2 * TILE_ROWS)
    ]
    codes_own = jnp.where((own >= 0) & (own < 16), -64, 0)
    for k in range(SLOTS):
        column = jnp.zeros((8, 128), jnp.int32)
        for t in range(2 * TILE_ROWS):
            column = jnp.where(row8 == t, target[t][k], column)
        codes_own = jnp.where(own == k, column, codes_own)
        codes_own = jnp.where(own == k + SLOTS, column + NBLK, codes_own)
    code[...] = codes_own
    codes[rep] = codes_own

    started = []

    class Sent:
        def __init__(self, src, dst, send, recv, device):
            self.copy = pltpu.make_async_remote_copy(
                src_ref=src, dst_ref=dst, send_sem=send, recv_sem=recv, device_id=device, device_id_type=MESH
            )

        def start(self):
            self.copy.start()
            started.append(self.copy)

        def wait_recv(self):
            self.copy.wait_recv()

    remote = Sent

    y_moves = ((3, 0, NX, 1), (5, 0, NX, -1), (4, 0, 2, 2), (4, 2, 2, -2), (2, 0, NX, 2), (6, 0, NX, -2), (1, 0, NX, 1), (7, 0, NX, -1))

    def y_slot(n):
        return y_slots.at[n, pl.ds(0, y_moves[n][2])]

    def y_copy(n):
        off, first, count, hops = y_moves[n]
        if n == 4 or n == 5:
            src = y_slot(n - 4)
        else:
            src = part.at[ORDER.index(off), pl.ds(first, count), pl.ds(0, H1)]
        return remote(src, y_slot(n), y_send.at[n], y_recv.at[n], (rep, at_y(hops)))

    def y_mid(side):
        first = y_moves[2 + side][1]
        y_copy(side).wait_recv()
        y_copy(2 + side).wait_recv()
        mine = part.at[ORDER.index(y_moves[4 + side][0])]
        near = slice(first, first + 2)
        rest = slice(2 - first, 4 - first)
        total = y_slots[side, near].astype(F32) + y_slots[2 + side, 0:2].astype(F32) + mine[near, 0:H1].astype(F32)
        y_slots[side, near] = total.astype(BF16)
        total = y_slots[side, rest].astype(F32) + mine[rest, 0:H1].astype(F32)
        y_slots[side, rest] = total.astype(BF16)
        y_copy(4 + side).start()

    def x_way(q):
        return 1 if q % 2 == 0 else -1

    def x_copy(q, which):
        way = x_way(q)
        n = 3 * q + which
        rows = pl.ds(2 * q, 2)
        if which == 0:
            src = part.at[rows, (x + 2) % NX, pl.ds(H1, H2)]
        elif which == 1:
            src = x_slots.at[3 * q]
        else:
            src = part.at[rows, (x - way) % NX, pl.ds(H1, H2)]
            way = -way
        return remote(src, x_slots.at[n], x_send.at[n], x_recv.at[n], (rep, at_x(way)))

    def x_mid(q):
        x_copy(q, 0).wait_recv()
        mine = part[2 * q : 2 * q + 2, (x + x_way(q)) % NX, H1:ROWS]
        x_slots[3 * q] = (x_slots[3 * q].astype(F32) + mine.astype(F32)).astype(BF16)
        x_copy(q, 1).start()

    def y2_copy(off):
        j = ORDER.index(off)
        return remote(r2.at[j], y2_slots.at[off - 1], y2_send.at[off - 1], y2_recv.at[off - 1], (rep, at_y(off)))

    def x_last(q):
        x_copy(q, 2).wait_recv()
        x_copy(q, 1).wait_recv()
        mine = part[2 * q : 2 * q + 2, x, H1:ROWS].astype(F32)
        total = mine + x_slots[3 * q + 1].astype(F32) + x_slots[3 * q + 2].astype(F32)
        r2[2 * q : 2 * q + 2] = total.astype(BF16)
        for off in ORDER[2 * q : 2 * q + 2]:
            if off:
                y2_copy(off).start()

    def x1_copy(off):
        return remote(
            r1.at[(x + off) % NX], x1_slots.at[off - 1], x1_send.at[off - 1], x1_recv.at[off - 1], (rep, at_x(off))
        )

    def c_copy(off):
        return remote(code, codes.at[rep], c_send.at[off - 1], c_recv.at[off - 1], (at_rep(off), pos))

    def g_copy(off):
        mine = listed.at[:, rep]
        return remote(mine, mine, g_send.at[off - 1], g_recv.at[off - 1], (at_rep(off), pos))

    u_copy.wait()
    grads = u_vm[...].T

    for q in range(STREAMS):
        load(2 * q).wait()
        load(2 * q + 1).wait()
        for j in range(2 * q, 2 * q + 2):
            columns = jnp.dot(grads, a_vm[j], preferred_element_type=F32).astype(BF16)
            part[j] = columns.T.reshape(NX, ROWS, FW)
        if q == 0:
            pl.semaphore_wait(barrier, NY - 1 + NX - 1 + NREP - 1)
            y_copy(0).start()
            y_copy(2).start()
            y_copy(3).start()
        if q == 1:
            y_copy(1).start()
        if q == 2:
            y_copy(6).start()
        if q == 3:
            y_copy(7).start()
        x_copy(q, 0).start()
        x_copy(q, 2).start()

    y_mid(0)
    y_mid(1)
    x_mid(0)
    x_mid(1)
    x_mid(2)
    x_mid(3)
    x_last(0)
    x_last(1)
    for off in range(1, NREP):
        c_copy(off).start()

    total = part[ORDER.index(0), :, 0:H1].astype(F32)
    for n in (6, 7, 4, 5):
        y_copy(n).wait_recv()
        total += y_slots[n].astype(F32)
    r1[...] = total.astype(BF16)
    for off in range(1, NX):
        x1_copy(off).start()
    x_last(2)
    x_last(3)

    for off in range(1, NREP):
        c_copy(off).wait_recv()
    row64 = lax.broadcasted_iota(jnp.int32, (EDGE, 128), 0)
    lane64 = lax.broadcasted_iota(jnp.int32, (EDGE, 128), 1)
    for side in range(NREP // 8):
        tile = codes[8 * side]
        for r in range(1, 8):
            tile += codes[8 * side + r]
        for t in range(2 * TILE_ROWS):
            hit = (tile[t : t + 1] == row64).astype(F32).astype(BF16)
            spread_w[t // 2, EDGE * (t % 2) : EDGE * (t % 2) + EDGE, 128 * side : 128 * side + 128] = hit

    for copy in others[2:]:
        copy.wait()

    g1 = r1[x].astype(F32)
    for off in range(1, NX):
        x1_copy(off).wait_recv()
        g1 += x1_slots[off - 1].astype(F32)
    moment_vm[0:H1] = 0.9 * mom_vm[0, 0:H1] + g1
    g2 = r2[ORDER.index(0)].astype(F32)
    for off in range(1, NY):
        y2_copy(off).wait_recv()
        g2 += y2_slots[off - 1].astype(F32)
    moment_vm[H1:ROWS] = 0.9 * mom_vm[0, H1:ROWS] + g2
    moment = moment_vm[...]

    def left(table, v):
        out = []
        for a in range(TILE_ROWS):
            hi, lo = parts_of(v[a * EDGE : a * EDGE + EDGE])
            out.append(dot(table, jnp.concatenate([hi, lo, hi], axis=0)))
        return jnp.concatenate(out, axis=0)

    hi, lo = parts_of(moment)
    coeffs = left(lf_vm[...], dot(jnp.concatenate([hi, lo, hi], axis=1), rf_vm[...])).astype(BF16).astype(F32)
    low_lanes = lane64 < EDGE
    block64 = row64 % NBLK
    keep = []
    stage[...] = jnp.zeros_like(stage)
    for a in range(TILE_ROWS):
        tile = coeffs[a * EDGE : a * EDGE + EDGE]
        live = jnp.zeros((EDGE, 128), F32)
        for k in range(SLOTS):
            chosen = jnp.where(low_lanes, target[2 * a][k], target[2 * a + 1][k]) == block64
            live = jnp.where(chosen, 1.0, live)
            rows = jnp.where(chosen, tile, 0.0)
            stage[a, k : k + 1] = jnp.sum(rows[0:NBLK], axis=0, keepdims=True)
            stage[a, SLOTS + k : SLOTS + k + 1] = jnp.sum(rows[NBLK:EDGE], axis=0, keepdims=True)
        keep.append(tile * live)
    listed[:, rep] = stage[...].astype(BF16)
    for off in range(1, NREP):
        g_copy(off).start()

    removed = jnp.concatenate(keep, axis=0).astype(BF16)
    right_inv = ri_vm[...]
    taken = left(li_vm[...], dot(jnp.concatenate([removed, removed], axis=1), right_inv[0:256]))
    out_ref[1] = moment - taken

    for copy in started:
        copy.wait_send()
    for off in range(1, NREP):
        g_copy(off).wait_recv()

    summed = []
    for a in range(TILE_ROWS):
        rows = dot(spread_w[a], listed[a].reshape(NREP * 16, 128))
        summed.append(jnp.where(low_lanes, rows[0:EDGE], rows[EDGE : 2 * EDGE]))
    hi, lo = parts_of(jnp.concatenate(summed, axis=0))
    update = left(li_vm[...], dot(jnp.concatenate([hi, hi, lo], axis=1), right_inv))
    lane1 = lax.broadcasted_iota(jnp.int32, (1, 128), 1) < EDGE
    for a in range(TILE_ROWS):
        tile = update[a * EDGE : a * EDGE + EDGE]
        squares = jnp.sum(tile * tile, axis=0, keepdims=True)
        first = jnp.sum(jnp.where(lane1, squares, 0.0), axis=1, keepdims=True)
        second = jnp.sum(jnp.where(lane1, 0.0, squares), axis=1, keepdims=True)
        scale = lax.rsqrt(jnp.where(lane1, first, second) * (1.0 / (EDGE * EDGE)) + 1e-6)
        span = slice(a * EDGE, a * EDGE + EDGE)
        out_ref[0, span] = w_vm[span] - 0.25 * jnp.tanh(tile * scale)


def on_device(activations, unit_grads, momentum, weights, block_ids, block_counts):
    right_fwd, right_inv, left_fwd, left_inv = tables()
    hbm = pl.BlockSpec(memory_space=pltpu.HBM)
    dma = pltpu.SemaphoreType.DMA
    both = pl.pallas_call(
        kernel,
        out_shape=pltpu.VMEM((2, ROWS, FW), F32),
        in_specs=[hbm] * 10,
        out_specs=pl.BlockSpec(memory_space=pltpu.VMEM),
        scratch_shapes=[
            pltpu.VMEM((NY, TOK, GROUP), BF16),
            pltpu.VMEM((TOK, FW), BF16),
            pltpu.VMEM((1, ROWS, FW), F32),
            pltpu.VMEM((ROWS, FW), F32),
            pltpu.VMEM(right_fwd.shape, BF16),
            pltpu.VMEM(right_inv.shape, BF16),
            pltpu.VMEM(left_fwd.shape, BF16),
            pltpu.VMEM(left_inv.shape, BF16),
            pltpu.SMEM((2 * TILE_ROWS, 1, SLOTS), jnp.int32),
            pltpu.SMEM((1, 2 * TILE_ROWS), jnp.int32),
            pltpu.VMEM((NY, NX, ROWS, FW), BF16),
            pltpu.VMEM((8, NX, H1, FW), BF16),
            pltpu.VMEM((3 * STREAMS, 2, H2, FW), BF16),
            pltpu.VMEM((NX, H1, FW), BF16),
            pltpu.VMEM((NY, H2, FW), BF16),
            pltpu.VMEM((NX - 1, H1, FW), BF16),
            pltpu.VMEM((NY - 1, H2, FW), BF16),
            pltpu.VMEM((8, 128), jnp.int32),
            pltpu.VMEM((NREP, 8, 128), jnp.int32),
            pltpu.VMEM((TILE_ROWS, 2 * EDGE, NREP * 16), BF16),
            pltpu.VMEM((TILE_ROWS, NREP, 16, 128), BF16),
            pltpu.VMEM((TILE_ROWS, 16, 128), F32),
            pltpu.VMEM((ROWS, FW), F32),
            dma((NY,)),
            dma((9,)),
            dma((8,)), dma((8,)),
            dma((3 * STREAMS,)), dma((3 * STREAMS,)),
            dma((NX - 1,)), dma((NX - 1,)),
            dma((NY - 1,)), dma((NY - 1,)),
            dma((NREP - 1,)), dma((NREP - 1,)),
            dma((NREP - 1,)), dma((NREP - 1,)),
        ],
        compiler_params=pltpu.CompilerParams(
            collective_id=0, has_side_effects=True, vmem_limit_bytes=60 * 1024 * 1024
        ),
    )(activations, unit_grads, momentum, weights, jnp.transpose(block_ids, (1, 0, 2)), block_counts, right_fwd, right_inv, left_fwd, left_inv)
    return both[0], both[1:2]


def solution(mesh):
    placed = (
        P(("rep", "fsdp"), None),
        P(("rep", "fsdp"), None),
        P("rep", "fsdp", None),
        P("fsdp", None),
        P("rep", "fsdp", None),
        P("rep", "fsdp"),
    )
    return jax.shard_map(
        on_device,
        mesh=mesh,
        in_specs=placed,
        out_specs=(P("fsdp", None), P("rep", "fsdp", None)),
        check_vma=False,
    )
```

```python
import functools

import jax
import jax.numpy as jnp
import ml_dtypes
import numpy as np
from jax import lax
from jax.experimental import pallas as pl
from jax.experimental.pallas import tpu as pltpu
from jax.sharding import PartitionSpec as P

MESH = pl.DeviceIdType.MESH
F32 = jnp.float32
BF16 = jnp.bfloat16

EDGE = 64
NBLK = 32
SLOTS = 6
FW = 128
NX, NY, NREP = 4, 8, 16
TILE_ROWS = 3
ROWS = TILE_ROWS * EDGE
GROUP = NX * ROWS
TOK = 256
H1 = 64
H2 = ROWS - H1
ORDER = (4, 3, 5, 2, 6, 1, 7, 0)
STREAMS = 4
REPLICAS = (8, 7, 9, 6, 10, 5, 11, 4, 12, 3, 13, 2, 14, 1, 15)
PIECES = (slice(0, 1), slice(1, 3))


def tables():
    freq = np.arange(EDGE)[:, None].astype(np.float64)
    place = np.arange(EDGE)[None, :].astype(np.float64)
    factor = np.where(freq == 0, np.sqrt(1.0 / EDGE), np.sqrt(2.0 / EDGE))
    table = (factor * np.cos(np.pi * (2.0 * place + 1.0) * freq / (2.0 * EDGE))).astype(np.float32)

    def halves(m):
        hi = m.astype(ml_dtypes.bfloat16)
        lo = (m - hi.astype(np.float32)).astype(ml_dtypes.bfloat16)
        return hi, lo

    both = np.zeros((2 * EDGE, 2 * EDGE), np.float32)
    both[:EDGE, :EDGE] = table
    both[EDGE:, EDGE:] = table
    split = np.concatenate([table[0::2], table[1::2]], axis=0)
    hi, lo = halves(both.T)
    right_fwd = np.concatenate([hi, hi, lo], axis=0)
    hi, lo = halves(both)
    right_inv = np.concatenate([hi, lo, hi], axis=0)
    hi, lo = halves(split)
    left_fwd = np.concatenate([hi, hi, lo], axis=1)
    hi, lo = halves(split.T)
    left_inv = np.concatenate([hi, hi, lo], axis=1)
    return right_fwd, right_inv, left_fwd, left_inv


def dot(a, b):
    return jnp.dot(a, b, preferred_element_type=F32)


def parts_of(v):
    hi = v.astype(BF16)
    lo = (v - hi.astype(F32)).astype(BF16)
    return hi, lo


def kernel(
    a_hbm, u_hbm, mom_hbm, w_hbm, ids_hbm, cnt_hbm, rf_hbm, ri_hbm, lf_hbm, li_hbm,
    out_ref,
    a_vm, u_vm, mom_vm, w_vm, rf_vm, ri_vm, lf_vm, li_vm,
    ids_ref, cnt_ref, part, y_slots, x_slots, r1, r2, x1_slots, y2_slots,
    code, codes, spread_w, listed, stage,
    load_sem, in_sem,
    y_send, y_recv, x_send, x_recv, x1_send, x1_recv, y2_send, y2_recv,
    c_send, c_recv, g_send, g_recv,
):
    rep = lax.axis_index("rep")
    pos = lax.axis_index("fsdp")
    y = pos // NX
    x = pos % NX

    def at_y(off):
        return ((y + off) % NY) * NX + x

    def at_x(off):
        return y * NX + (x + off) % NX

    def at_rep(off):
        return (rep + off) % NREP

    barrier = pltpu.get_barrier_semaphore()
    for off in range(1, NY):
        pl.semaphore_signal(barrier, inc=1, device_id=(rep, at_y(off)), device_id_type=MESH)
    for off in range(1, NX):
        pl.semaphore_signal(barrier, inc=1, device_id=(rep, at_x(off)), device_id_type=MESH)

    def load(j):
        t = (y + ORDER[j]) % NY
        cols = pl.ds(pl.multiple_of(t * GROUP, GROUP), GROUP)
        return pltpu.make_async_copy(a_hbm.at[:, cols], a_vm.at[j], load_sem.at[j])

    u_copy = pltpu.make_async_copy(u_hbm, u_vm, in_sem.at[0])
    others = [
        pltpu.make_async_copy(src, dst, in_sem.at[n + 1])
        for n, (src, dst) in enumerate(
            [(ids_hbm, ids_ref), (cnt_hbm, cnt_ref), (mom_hbm, mom_vm), (w_hbm, w_vm), (rf_hbm, rf_vm), (ri_hbm, ri_vm), (lf_hbm, lf_vm), (li_hbm, li_vm)]
        )
    ]
    for copy in others[0:2]:
        copy.start()
    u_copy.start()
    for j in range(2):
        load(j).start()

    for off in range(1, NREP):
        pl.semaphore_signal(barrier, inc=1, device_id=(at_rep(off), pos), device_id_type=MESH)

    for j in range(2, NY):
        load(j).start()
    for copy in others[2:]:
        copy.start()

    started = []

    class Sent:
        def __init__(self, src, dst, send, recv, device):
            self.copy = pltpu.make_async_remote_copy(
                src_ref=src, dst_ref=dst, send_sem=send, recv_sem=recv, device_id=device, device_id_type=MESH
            )

        def start(self):
            self.copy.start()
            started.append(self.copy)

        def wait_recv(self):
            self.copy.wait_recv()

    remote = Sent

    y_moves = ((3, 0, NX, 1), (5, 0, NX, -1), (4, 0, 2, 2), (4, 2, 2, -2), (2, 0, NX, 2), (6, 0, NX, -2), (1, 0, NX, 1), (7, 0, NX, -1))

    def y_slot(n):
        return y_slots.at[n, pl.ds(0, y_moves[n][2])]

    def y_copy(n):
        off, first, count, hops = y_moves[n]
        if n == 4 or n == 5:
            src = y_slot(n - 4)
        else:
            src = part.at[ORDER.index(off), pl.ds(first, count), pl.ds(0, H1)]
        return remote(src, y_slot(n), y_send.at[n], y_recv.at[n], (rep, at_y(hops)))

    def y_mid(side):
        first = y_moves[2 + side][1]
        y_copy(side).wait_recv()
        y_copy(2 + side).wait_recv()
        mine = part.at[ORDER.index(y_moves[4 + side][0])]
        near = slice(first, first + 2)
        rest = slice(2 - first, 4 - first)
        total = y_slots[side, near].astype(F32) + y_slots[2 + side, 0:2].astype(F32) + mine[near, 0:H1].astype(F32)
        y_slots[side, near] = total.astype(BF16)
        total = y_slots[side, rest].astype(F32) + mine[rest, 0:H1].astype(F32)
        y_slots[side, rest] = total.astype(BF16)
        y_copy(4 + side).start()

    def x_way(q):
        return 1 if q % 2 == 0 else -1

    def x_copy(q, which):
        way = x_way(q)
        n = 3 * q + which
        rows = pl.ds(2 * q, 2)
        if which == 0:
            src = part.at[rows, (x + 2) % NX, pl.ds(H1, H2)]
        elif which == 1:
            src = x_slots.at[3 * q]
        else:
            src = part.at[rows, (x - way) % NX, pl.ds(H1, H2)]
            way = -way
        return remote(src, x_slots.at[n], x_send.at[n], x_recv.at[n], (rep, at_x(way)))

    def x_mid(q):
        x_copy(q, 0).wait_recv()
        mine = part[2 * q : 2 * q + 2, (x + x_way(q)) % NX, H1:ROWS]
        x_slots[3 * q] = (x_slots[3 * q].astype(F32) + mine.astype(F32)).astype(BF16)
        x_copy(q, 1).start()

    def y2_copy(off):
        j = ORDER.index(off)
        return remote(r2.at[j], y2_slots.at[off - 1], y2_send.at[off - 1], y2_recv.at[off - 1], (rep, at_y(off)))

    def x_last(q):
        x_copy(q, 2).wait_recv()
        x_copy(q, 1).wait_recv()
        mine = part[2 * q : 2 * q + 2, x, H1:ROWS].astype(F32)
        total = mine + x_slots[3 * q + 1].astype(F32) + x_slots[3 * q + 2].astype(F32)
        r2[2 * q : 2 * q + 2] = total.astype(BF16)
        for off in ORDER[2 * q : 2 * q + 2]:
            if off:
                y2_copy(off).start()

    def x1_copy(off):
        return remote(
            r1.at[(x + off) % NX], x1_slots.at[off - 1], x1_send.at[off - 1], x1_recv.at[off - 1], (rep, at_x(off))
        )

    def c_copy(off):
        return remote(code, codes.at[rep], c_send.at[off - 1], c_recv.at[off - 1], (at_rep(off), pos))

    def g_copy(piece, off):
        n = piece * (NREP - 1) + off - 1
        mine = listed.at[PIECES[piece], rep]
        return remote(mine, mine, g_send.at[n], g_recv.at[n], (at_rep(off), pos))

    u_copy.wait()
    grads = u_vm[...].T

    for q in range(STREAMS):
        load(2 * q).wait()
        load(2 * q + 1).wait()
        for j in range(2 * q, 2 * q + 2):
            columns = jnp.dot(grads, a_vm[j], preferred_element_type=F32).astype(BF16)
            part[j] = columns.T.reshape(NX, ROWS, FW)
        if q == 0:
            pl.semaphore_wait(barrier, NY - 1 + NX - 1 + NREP - 1)
            y_copy(0).start()
            y_copy(2).start()
            y_copy(3).start()
        if q == 1:
            y_copy(1).start()
        if q == 2:
            y_copy(6).start()
        if q == 3:
            y_copy(7).start()
        x_copy(q, 0).start()
        x_copy(q, 2).start()

    for copy in others[0:2]:
        copy.wait()
    lane8 = lax.broadcasted_iota(jnp.int32, (8, 128), 1)
    row8 = lax.broadcasted_iota(jnp.int32, (8, 128), 0)
    own = lane8 - (rep % 8) * 16
    target = [
        [jnp.where(k < cnt_ref[0, t], ids_ref[t, 0, k], -64) for k in range(SLOTS)] for t in range(2 * TILE_ROWS)
    ]
    codes_own = jnp.where((own >= 0) & (own < 16), -64, 0)
    for k in range(SLOTS):
        column = jnp.zeros((8, 128), jnp.int32)
        for t in range(2 * TILE_ROWS):
            column = jnp.where(row8 == t, target[t][k], column)
        codes_own = jnp.where(own == k, column, codes_own)
        codes_own = jnp.where(own == k + SLOTS, column + NBLK, codes_own)
    code[...] = codes_own
    codes[rep] = codes_own
    stage[...] = jnp.zeros_like(stage)

    y_mid(0)
    y_mid(1)
    x_mid(0)
    x_mid(1)
    x_mid(2)
    x_mid(3)
    x_last(0)
    x_last(1)

    total = part[ORDER.index(0), :, 0:H1].astype(F32)
    for n in (6, 7, 4, 5):
        y_copy(n).wait_recv()
        total += y_slots[n].astype(F32)
    r1[...] = total.astype(BF16)
    for off in range(1, NX):
        x1_copy(off).start()
    x_last(2)
    x_last(3)
    for off in range(1, NREP):
        c_copy(off).start()

    for copy in others[2:]:
        copy.wait()

    row64 = lax.broadcasted_iota(jnp.int32, (EDGE, 128), 0)
    lane64 = lax.broadcasted_iota(jnp.int32, (EDGE, 128), 1)
    low_lanes = lane64 < EDGE
    block64 = row64 % NBLK

    def left(table, v):
        out = []
        for a in range(v.shape[0] // EDGE):
            hi, lo = parts_of(v[a * EDGE : a * EDGE + EDGE])
            out.append(dot(table, jnp.concatenate([hi, lo, hi], axis=0)))
        return jnp.concatenate(out, axis=0)

    keep = []

    def list_and_send(piece, moment):
        hi, lo = parts_of(moment)
        coeffs = left(lf_vm[...], dot(jnp.concatenate([hi, lo, hi], axis=1), rf_vm[...])).astype(BF16).astype(F32)
        first = PIECES[piece].start
        for a in range(first, PIECES[piece].stop):
            tile = coeffs[(a - first) * EDGE : (a - first) * EDGE + EDGE]
            live = jnp.zeros((EDGE, 128), F32)
            for k in range(SLOTS):
                chosen = jnp.where(low_lanes, target[2 * a][k], target[2 * a + 1][k]) == block64
                live = jnp.where(chosen, 1.0, live)
                rows = jnp.where(chosen, tile, 0.0)
                stage[a, k : k + 1] = jnp.sum(rows[0:NBLK], axis=0, keepdims=True)
                stage[a, SLOTS + k : SLOTS + k + 1] = jnp.sum(rows[NBLK:EDGE], axis=0, keepdims=True)
            keep.append(tile * live)
            listed[a, rep] = stage[a].astype(BF16)
        for off in REPLICAS:
            g_copy(piece, off).start()

    g1 = r1[x].astype(F32)
    for off in range(1, NX):
        x1_copy(off).wait_recv()
        g1 += x1_slots[off - 1].astype(F32)
    moment1 = 0.9 * mom_vm[0, 0:H1] + g1
    list_and_send(0, moment1)
    g2 = r2[ORDER.index(0)].astype(F32)
    for off in range(1, NY):
        y2_copy(off).wait_recv()
        g2 += y2_slots[off - 1].astype(F32)
    moment2 = 0.9 * mom_vm[0, H1:ROWS] + g2
    list_and_send(1, moment2)

    removed = jnp.concatenate(keep, axis=0).astype(BF16)
    right_inv = ri_vm[...]
    taken = left(li_vm[...], dot(jnp.concatenate([removed, removed], axis=1), right_inv[0:256]))
    out_ref[1, 0:H1] = moment1 - taken[0:H1]
    out_ref[1, H1:ROWS] = moment2 - taken[H1:ROWS]

    for off in range(1, NREP):
        c_copy(off).wait_recv()
    for side in range(NREP // 8):
        tile = codes[8 * side]
        for r in range(1, 8):
            tile += codes[8 * side + r]
        for t in range(2 * TILE_ROWS):
            hit = (tile[t : t + 1] == row64).astype(F32).astype(BF16)
            spread_w[t // 2, EDGE * (t % 2) : EDGE * (t % 2) + EDGE, 128 * side : 128 * side + 128] = hit

    for copy in started:
        copy.wait_send()
    for piece in range(len(PIECES)):
        for off in range(1, NREP):
            g_copy(piece, off).wait_recv()

    summed = []
    for a in range(TILE_ROWS):
        rows = dot(spread_w[a], listed[a].reshape(NREP * 16, 128))
        summed.append(jnp.where(low_lanes, rows[0:EDGE], rows[EDGE : 2 * EDGE]))
    hi, lo = parts_of(jnp.concatenate(summed, axis=0))
    update = left(li_vm[...], dot(jnp.concatenate([hi, hi, lo], axis=1), right_inv))
    lane1 = lax.broadcasted_iota(jnp.int32, (1, 128), 1) < EDGE
    for a in range(TILE_ROWS):
        tile = update[a * EDGE : a * EDGE + EDGE]
        squares = jnp.sum(tile * tile, axis=0, keepdims=True)
        first = jnp.sum(jnp.where(lane1, squares, 0.0), axis=1, keepdims=True)
        second = jnp.sum(jnp.where(lane1, 0.0, squares), axis=1, keepdims=True)
        scale = lax.rsqrt(jnp.where(lane1, first, second) * (1.0 / (EDGE * EDGE)) + 1e-6)
        span = slice(a * EDGE, a * EDGE + EDGE)
        out_ref[0, span] = w_vm[span] - 0.25 * jnp.tanh(tile * scale)


def on_device(activations, unit_grads, momentum, weights, block_ids, block_counts):
    right_fwd, right_inv, left_fwd, left_inv = tables()
    hbm = pl.BlockSpec(memory_space=pltpu.HBM)
    dma = pltpu.SemaphoreType.DMA
    both = pl.pallas_call(
        kernel,
        out_shape=pltpu.VMEM((2, ROWS, FW), F32),
        in_specs=[hbm] * 10,
        out_specs=pl.BlockSpec(memory_space=pltpu.VMEM),
        scratch_shapes=[
            pltpu.VMEM((NY, TOK, GROUP), BF16),
            pltpu.VMEM((TOK, FW), BF16),
            pltpu.VMEM((1, ROWS, FW), F32),
            pltpu.VMEM((ROWS, FW), F32),
            pltpu.VMEM(right_fwd.shape, BF16),
            pltpu.VMEM(right_inv.shape, BF16),
            pltpu.VMEM(left_fwd.shape, BF16),
            pltpu.VMEM(left_inv.shape, BF16),
            pltpu.SMEM((2 * TILE_ROWS, 1, SLOTS), jnp.int32),
            pltpu.SMEM((1, 2 * TILE_ROWS), jnp.int32),
            pltpu.VMEM((NY, NX, ROWS, FW), BF16),
            pltpu.VMEM((8, NX, H1, FW), BF16),
            pltpu.VMEM((3 * STREAMS, 2, H2, FW), BF16),
            pltpu.VMEM((NX, H1, FW), BF16),
            pltpu.VMEM((NY, H2, FW), BF16),
            pltpu.VMEM((NX - 1, H1, FW), BF16),
            pltpu.VMEM((NY - 1, H2, FW), BF16),
            pltpu.VMEM((8, 128), jnp.int32),
            pltpu.VMEM((NREP, 8, 128), jnp.int32),
            pltpu.VMEM((TILE_ROWS, 2 * EDGE, NREP * 16), BF16),
            pltpu.VMEM((TILE_ROWS, NREP, 16, 128), BF16),
            pltpu.VMEM((TILE_ROWS, 16, 128), F32),
            dma((NY,)),
            dma((9,)),
            dma((8,)), dma((8,)),
            dma((3 * STREAMS,)), dma((3 * STREAMS,)),
            dma((NX - 1,)), dma((NX - 1,)),
            dma((NY - 1,)), dma((NY - 1,)),
            dma((NREP - 1,)), dma((NREP - 1,)),
            dma((len(PIECES) * (NREP - 1),)), dma((len(PIECES) * (NREP - 1),)),
        ],
        compiler_params=pltpu.CompilerParams(
            collective_id=0, has_side_effects=True, vmem_limit_bytes=60 * 1024 * 1024
        ),
    )(activations, unit_grads, momentum, weights, jnp.transpose(block_ids, (1, 0, 2)), block_counts, right_fwd, right_inv, left_fwd, left_inv)
    return both[0], both[1:2]


def solution(mesh):
    placed = (
        P(("rep", "fsdp"), None),
        P(("rep", "fsdp"), None),
        P("rep", "fsdp", None),
        P("fsdp", None),
        P("rep", "fsdp", None),
        P("rep", "fsdp"),
    )
    return jax.shard_map(
        on_device,
        mesh=mesh,
        in_specs=placed,
        out_specs=(P("fsdp", None), P("rep", "fsdp", None)),
        check_vma=False,
    )
```

```python
import functools

import jax
import jax.numpy as jnp
import ml_dtypes
import numpy as np
from jax import lax
from jax.experimental import pallas as pl
from jax.experimental.pallas import tpu as pltpu
from jax.sharding import PartitionSpec as P

MESH = pl.DeviceIdType.MESH
F32 = jnp.float32
BF16 = jnp.bfloat16

EDGE = 64
NBLK = 32
SLOTS = 6
FW = 128
NX, NY, NREP = 4, 8, 16
TILE_ROWS = 3
ROWS = TILE_ROWS * EDGE
GROUP = NX * ROWS
TOK = 256
H1 = 64
H2 = ROWS - H1
ORDER = (4, 3, 5, 2, 6, 1, 7, 0)
STREAMS = 4
REPLICAS = (8, 7, 9, 6, 10, 5, 11, 4, 12, 3, 13, 2, 14, 1, 15)
PIECES = (slice(0, 1), slice(1, 3))


def tables():
    freq = np.arange(EDGE)[:, None].astype(np.float64)
    place = np.arange(EDGE)[None, :].astype(np.float64)
    factor = np.where(freq == 0, np.sqrt(1.0 / EDGE), np.sqrt(2.0 / EDGE))
    table = (factor * np.cos(np.pi * (2.0 * place + 1.0) * freq / (2.0 * EDGE))).astype(np.float32)

    def halves(m):
        hi = m.astype(ml_dtypes.bfloat16)
        lo = (m - hi.astype(np.float32)).astype(ml_dtypes.bfloat16)
        return hi, lo

    both = np.zeros((2 * EDGE, 2 * EDGE), np.float32)
    both[:EDGE, :EDGE] = table
    both[EDGE:, EDGE:] = table
    split = np.concatenate([table[0::2], table[1::2]], axis=0)
    hi, lo = halves(both.T)
    right_fwd = np.concatenate([hi, hi, lo], axis=0)
    hi, lo = halves(both)
    right_inv = np.concatenate([hi, lo, hi], axis=0)
    hi, lo = halves(split)
    left_fwd = np.concatenate([hi, hi, lo], axis=1)
    hi, lo = halves(split.T)
    left_inv = np.concatenate([hi, hi, lo], axis=1)
    return right_fwd, right_inv, left_fwd, left_inv


def dot(a, b):
    return jnp.dot(a, b, preferred_element_type=F32)


def parts_of(v):
    hi = v.astype(BF16)
    lo = (v - hi.astype(F32)).astype(BF16)
    return hi, lo


def kernel(
    a_hbm, u_hbm, mom_hbm, w_hbm, ids_hbm, cnt_hbm, rf_hbm, ri_hbm, lf_hbm, li_hbm,
    out_ref,
    a_vm, u_vm, mom_vm, w_vm, rf_vm, ri_vm, lf_vm, li_vm,
    ids_ref, cnt_ref, part, y_slots, x_slots, r1, r2, x1_slots, y2_slots,
    code, codes, spread_w, listed, stage,
    load_sem, in_sem,
    y_send, y_recv, x_send, x_recv, x1_send, x1_recv, y2_send, y2_recv,
    c_send, c_recv, g_send, g_recv,
):
    rep = lax.axis_index("rep")
    pos = lax.axis_index("fsdp")
    y = pos // NX
    x = pos % NX

    def at_y(off):
        return ((y + off) % NY) * NX + x

    def at_x(off):
        return y * NX + (x + NX + off) % NX

    def at_rep(off):
        return (rep + off) % NREP

    barrier = pltpu.get_barrier_semaphore()
    for off in range(1, NY):
        pl.semaphore_signal(barrier, inc=1, device_id=(rep, at_y(off)), device_id_type=MESH)
    for off in range(1, NX):
        pl.semaphore_signal(barrier, inc=1, device_id=(rep, at_x(off)), device_id_type=MESH)

    def load(j):
        t = (y + ORDER[j]) % NY
        cols = pl.ds(pl.multiple_of(t * GROUP, GROUP), GROUP)
        return pltpu.make_async_copy(a_hbm.at[:, cols], a_vm.at[j], load_sem.at[j])

    u_copy = pltpu.make_async_copy(u_hbm, u_vm, in_sem.at[0])
    others = [
        pltpu.make_async_copy(src, dst, in_sem.at[n + 1])
        for n, (src, dst) in enumerate(
            [(ids_hbm, ids_ref), (cnt_hbm, cnt_ref), (mom_hbm, mom_vm), (w_hbm, w_vm), (rf_hbm, rf_vm), (ri_hbm, ri_vm), (lf_hbm, lf_vm), (li_hbm, li_vm)]
        )
    ]
    for copy in others[0:2]:
        copy.start()
    u_copy.start()
    for j in range(2):
        load(j).start()

    for off in range(1, NREP):
        pl.semaphore_signal(barrier, inc=1, device_id=(at_rep(off), pos), device_id_type=MESH)

    for j in range(2, NY):
        load(j).start()
    for copy in others[2:]:
        copy.start()

    started = []

    class Sent:
        def __init__(self, src, dst, send, recv, device):
            self.copy = pltpu.make_async_remote_copy(
                src_ref=src, dst_ref=dst, send_sem=send, recv_sem=recv, device_id=device, device_id_type=MESH
            )

        def start(self):
            self.copy.start()
            started.append(self.copy)

        def wait_recv(self):
            self.copy.wait_recv()

    remote = Sent

    y_moves = ((3, 0, NX, 1), (5, 0, NX, -1), (4, 0, 2, 2), (4, 2, 2, -2), (2, 0, NX, 2), (6, 0, NX, -2), (1, 0, NX, 1), (7, 0, NX, -1))

    def y_slot(n):
        return y_slots.at[n, pl.ds(0, y_moves[n][2])]

    def y_copy(n):
        off, first, count, hops = y_moves[n]
        if n == 4 or n == 5:
            src = y_slot(n - 4)
        else:
            src = part.at[ORDER.index(off), pl.ds(first, count), pl.ds(0, H1)]
        return remote(src, y_slot(n), y_send.at[n], y_recv.at[n], (rep, at_y(hops)))

    def y_mid(side):
        first = y_moves[2 + side][1]
        y_copy(side).wait_recv()
        y_copy(2 + side).wait_recv()
        mine = part.at[ORDER.index(y_moves[4 + side][0])]
        near = slice(first, first + 2)
        rest = slice(2 - first, 4 - first)
        total = y_slots[side, near].astype(F32) + y_slots[2 + side, 0:2].astype(F32) + mine[near, 0:H1].astype(F32)
        y_slots[side, near] = total.astype(BF16)
        total = y_slots[side, rest].astype(F32) + mine[rest, 0:H1].astype(F32)
        y_slots[side, rest] = total.astype(BF16)
        y_copy(4 + side).start()

    def x_way(q):
        return 1 - 2 * ((q + rep) % 2)

    def x_copy(q, which):
        way = x_way(q)
        n = 3 * q + which
        rows = pl.ds(2 * q, 2)
        if which == 0:
            src = part.at[rows, (x + 2) % NX, pl.ds(H1, H2)]
        elif which == 1:
            src = x_slots.at[3 * q]
        else:
            src = part.at[rows, (x + NX - way) % NX, pl.ds(H1, H2)]
            way = -way
        return remote(src, x_slots.at[n], x_send.at[n], x_recv.at[n], (rep, at_x(way)))

    def x_mid(q):
        x_copy(q, 0).wait_recv()
        mine = part[2 * q : 2 * q + 2, (x + NX + x_way(q)) % NX, H1:ROWS]
        x_slots[3 * q] = (x_slots[3 * q].astype(F32) + mine.astype(F32)).astype(BF16)
        x_copy(q, 1).start()

    def y2_copy(off):
        j = ORDER.index(off)
        return remote(r2.at[j], y2_slots.at[off - 1], y2_send.at[off - 1], y2_recv.at[off - 1], (rep, at_y(off)))

    def x_last(q):
        x_copy(q, 2).wait_recv()
        x_copy(q, 1).wait_recv()
        mine = part[2 * q : 2 * q + 2, x, H1:ROWS].astype(F32)
        total = mine + x_slots[3 * q + 1].astype(F32) + x_slots[3 * q + 2].astype(F32)
        r2[2 * q : 2 * q + 2] = total.astype(BF16)
        for off in ORDER[2 * q : 2 * q + 2]:
            if off:
                y2_copy(off).start()

    def x1_copy(off):
        return remote(
            r1.at[(x + off) % NX], x1_slots.at[off - 1], x1_send.at[off - 1], x1_recv.at[off - 1], (rep, at_x(off))
        )

    def c_copy(off):
        return remote(code, codes.at[rep], c_send.at[off - 1], c_recv.at[off - 1], (at_rep(off), pos))

    def g_copy(piece, off):
        n = piece * (NREP - 1) + off - 1
        mine = listed.at[PIECES[piece], rep]
        return remote(mine, mine, g_send.at[n], g_recv.at[n], (at_rep(off), pos))

    u_copy.wait()
    grads = u_vm[...].T

    for q in range(STREAMS):
        load(2 * q).wait()
        load(2 * q + 1).wait()
        for j in range(2 * q, 2 * q + 2):
            columns = jnp.dot(grads, a_vm[j], preferred_element_type=F32).astype(BF16)
            part[j] = columns.T.reshape(NX, ROWS, FW)
        if q == 0:
            pl.semaphore_wait(barrier, NY - 1 + NX - 1 + NREP - 1)
            y_copy(0).start()
            y_copy(2).start()
            y_copy(3).start()
        if q == 1:
            y_copy(1).start()
        if q == 2:
            y_copy(6).start()
        if q == 3:
            y_copy(7).start()
        x_copy(q, 0).start()
        x_copy(q, 2).start()

    for copy in others[0:2]:
        copy.wait()
    lane8 = lax.broadcasted_iota(jnp.int32, (8, 128), 1)
    row8 = lax.broadcasted_iota(jnp.int32, (8, 128), 0)
    own = lane8 - (rep % 8) * 16
    target = [
        [jnp.where(k < cnt_ref[0, t], ids_ref[t, 0, k], -64) for k in range(SLOTS)] for t in range(2 * TILE_ROWS)
    ]
    codes_own = jnp.where((own >= 0) & (own < 16), -64, 0)
    for k in range(SLOTS):
        column = jnp.zeros((8, 128), jnp.int32)
        for t in range(2 * TILE_ROWS):
            column = jnp.where(row8 == t, target[t][k], column)
        codes_own = jnp.where(own == k, column, codes_own)
        codes_own = jnp.where(own == k + SLOTS, column + NBLK, codes_own)
    code[...] = codes_own
    codes[rep] = codes_own
    stage[...] = jnp.zeros_like(stage)

    y_mid(0)
    y_mid(1)
    x_mid(0)
    x_mid(1)
    x_mid(2)
    x_mid(3)
    x_last(0)
    x_last(1)

    total = part[ORDER.index(0), :, 0:H1].astype(F32)
    for n in (6, 7, 4, 5):
        y_copy(n).wait_recv()
        total += y_slots[n].astype(F32)
    r1[...] = total.astype(BF16)
    for off in range(1, NX):
        x1_copy(off).start()
    x_last(2)
    x_last(3)
    for off in range(1, NREP):
        c_copy(off).start()

    for copy in others[2:]:
        copy.wait()

    row64 = lax.broadcasted_iota(jnp.int32, (EDGE, 128), 0)
    lane64 = lax.broadcasted_iota(jnp.int32, (EDGE, 128), 1)
    low_lanes = lane64 < EDGE
    block64 = row64 % NBLK

    def left(table, v):
        out = []
        for a in range(v.shape[0] // EDGE):
            hi, lo = parts_of(v[a * EDGE : a * EDGE + EDGE])
            out.append(dot(table, jnp.concatenate([hi, lo, hi], axis=0)))
        return jnp.concatenate(out, axis=0)

    keep = []

    def list_and_send(piece, moment):
        hi, lo = parts_of(moment)
        coeffs = left(lf_vm[...], dot(jnp.concatenate([hi, lo, hi], axis=1), rf_vm[...])).astype(BF16).astype(F32)
        first = PIECES[piece].start
        for a in range(first, PIECES[piece].stop):
            tile = coeffs[(a - first) * EDGE : (a - first) * EDGE + EDGE]
            live = jnp.zeros((EDGE, 128), F32)
            for k in range(SLOTS):
                chosen = jnp.where(low_lanes, target[2 * a][k], target[2 * a + 1][k]) == block64
                live = jnp.where(chosen, 1.0, live)
                rows = jnp.where(chosen, tile, 0.0)
                stage[a, k : k + 1] = jnp.sum(rows[0:NBLK], axis=0, keepdims=True)
                stage[a, SLOTS + k : SLOTS + k + 1] = jnp.sum(rows[NBLK:EDGE], axis=0, keepdims=True)
            keep.append(tile * live)
            listed[a, rep] = stage[a].astype(BF16)
        for off in REPLICAS:
            g_copy(piece, off).start()

    g1 = r1[x].astype(F32)
    for off in range(1, NX):
        x1_copy(off).wait_recv()
        g1 += x1_slots[off - 1].astype(F32)
    moment1 = 0.9 * mom_vm[0, 0:H1] + g1
    list_and_send(0, moment1)
    g2 = r2[ORDER.index(0)].astype(F32)
    for off in range(1, NY):
        y2_copy(off).wait_recv()
        g2 += y2_slots[off - 1].astype(F32)
    moment2 = 0.9 * mom_vm[0, H1:ROWS] + g2
    list_and_send(1, moment2)

    removed = jnp.concatenate(keep, axis=0).astype(BF16)
    right_inv = ri_vm[...]
    taken = left(li_vm[...], dot(jnp.concatenate([removed, removed], axis=1), right_inv[0:256]))
    out_ref[1, 0:H1] = moment1 - taken[0:H1]
    out_ref[1, H1:ROWS] = moment2 - taken[H1:ROWS]

    for off in range(1, NREP):
        c_copy(off).wait_recv()
    for side in range(NREP // 8):
        tile = codes[8 * side]
        for r in range(1, 8):
            tile += codes[8 * side + r]
        for t in range(2 * TILE_ROWS):
            hit = (tile[t : t + 1] == row64).astype(F32).astype(BF16)
            spread_w[t // 2, EDGE * (t % 2) : EDGE * (t % 2) + EDGE, 128 * side : 128 * side + 128] = hit

    for copy in started:
        copy.wait_send()
    lane1 = lax.broadcasted_iota(jnp.int32, (1, 128), 1) < EDGE
    for piece in range(len(PIECES)):
        for off in range(1, NREP):
            g_copy(piece, off).wait_recv()
        first = PIECES[piece].start
        summed = []
        for a in range(first, PIECES[piece].stop):
            rows = dot(spread_w[a], listed[a].reshape(NREP * 16, 128))
            summed.append(jnp.where(low_lanes, rows[0:EDGE], rows[EDGE : 2 * EDGE]))
        hi, lo = parts_of(jnp.concatenate(summed, axis=0))
        update = left(li_vm[...], dot(jnp.concatenate([hi, hi, lo], axis=1), right_inv))
        for a in range(first, PIECES[piece].stop):
            tile = update[(a - first) * EDGE : (a - first) * EDGE + EDGE]
            squares = jnp.sum(tile * tile, axis=0, keepdims=True)
            low = jnp.sum(jnp.where(lane1, squares, 0.0), axis=1, keepdims=True)
            high = jnp.sum(jnp.where(lane1, 0.0, squares), axis=1, keepdims=True)
            scale = lax.rsqrt(jnp.where(lane1, low, high) * (1.0 / (EDGE * EDGE)) + 1e-6)
            span = slice(a * EDGE, a * EDGE + EDGE)
            out_ref[0, span] = w_vm[span] - 0.25 * jnp.tanh(tile * scale)


def on_device(activations, unit_grads, momentum, weights, block_ids, block_counts):
    right_fwd, right_inv, left_fwd, left_inv = tables()
    hbm = pl.BlockSpec(memory_space=pltpu.HBM)
    dma = pltpu.SemaphoreType.DMA
    both = pl.pallas_call(
        kernel,
        out_shape=pltpu.VMEM((2, ROWS, FW), F32),
        in_specs=[hbm] * 10,
        out_specs=pl.BlockSpec(memory_space=pltpu.VMEM),
        scratch_shapes=[
            pltpu.VMEM((NY, TOK, GROUP), BF16),
            pltpu.VMEM((TOK, FW), BF16),
            pltpu.VMEM((1, ROWS, FW), F32),
            pltpu.VMEM((ROWS, FW), F32),
            pltpu.VMEM(right_fwd.shape, BF16),
            pltpu.VMEM(right_inv.shape, BF16),
            pltpu.VMEM(left_fwd.shape, BF16),
            pltpu.VMEM(left_inv.shape, BF16),
            pltpu.SMEM((2 * TILE_ROWS, 1, SLOTS), jnp.int32),
            pltpu.SMEM((1, 2 * TILE_ROWS), jnp.int32),
            pltpu.VMEM((NY, NX, ROWS, FW), BF16),
            pltpu.VMEM((8, NX, H1, FW), BF16),
            pltpu.VMEM((3 * STREAMS, 2, H2, FW), BF16),
            pltpu.VMEM((NX, H1, FW), BF16),
            pltpu.VMEM((NY, H2, FW), BF16),
            pltpu.VMEM((NX - 1, H1, FW), BF16),
            pltpu.VMEM((NY - 1, H2, FW), BF16),
            pltpu.VMEM((8, 128), jnp.int32),
            pltpu.VMEM((NREP, 8, 128), jnp.int32),
            pltpu.VMEM((TILE_ROWS, 2 * EDGE, NREP * 16), BF16),
            pltpu.VMEM((TILE_ROWS, NREP, 16, 128), BF16),
            pltpu.VMEM((TILE_ROWS, 16, 128), F32),
            dma((NY,)),
            dma((9,)),
            dma((8,)), dma((8,)),
            dma((3 * STREAMS,)), dma((3 * STREAMS,)),
            dma((NX - 1,)), dma((NX - 1,)),
            dma((NY - 1,)), dma((NY - 1,)),
            dma((NREP - 1,)), dma((NREP - 1,)),
            dma((len(PIECES) * (NREP - 1),)), dma((len(PIECES) * (NREP - 1),)),
        ],
        compiler_params=pltpu.CompilerParams(
            collective_id=0, has_side_effects=True, vmem_limit_bytes=60 * 1024 * 1024
        ),
    )(activations, unit_grads, momentum, weights, jnp.transpose(block_ids, (1, 0, 2)), block_counts, right_fwd, right_inv, left_fwd, left_inv)
    return both[0], both[1:2]


def solution(mesh):
    placed = (
        P(("rep", "fsdp"), None),
        P(("rep", "fsdp"), None),
        P("rep", "fsdp", None),
        P("fsdp", None),
        P("rep", "fsdp", None),
        P("rep", "fsdp"),
    )
    return jax.shard_map(
        on_device,
        mesh=mesh,
        in_specs=placed,
        out_specs=(P("fsdp", None), P("rep", "fsdp", None)),
        check_vma=False,
    )
```

```python
import functools

import jax
import jax.numpy as jnp
import ml_dtypes
import numpy as np
from jax import lax
from jax.experimental import pallas as pl
from jax.experimental.pallas import tpu as pltpu
from jax.sharding import PartitionSpec as P

MESH = pl.DeviceIdType.MESH
F32 = jnp.float32
BF16 = jnp.bfloat16

EDGE = 64
NBLK = 32
SLOTS = 6
FW = 128
NX, NY, NREP = 4, 8, 16
TILE_ROWS = 3
ROWS = TILE_ROWS * EDGE
GROUP = NX * ROWS
TOK = 256
H1 = 64
H2 = ROWS - H1
ORDER = (4, 3, 5, 2, 6, 1, 7, 0)
STREAMS = 4
REPLICAS = (8, 7, 9, 6, 10, 5, 11, 4, 12, 3, 13, 2, 14, 1, 15)
PIECES = (slice(0, 1), slice(1, 3))


def tables():
    freq = np.arange(EDGE)[:, None].astype(np.float64)
    place = np.arange(EDGE)[None, :].astype(np.float64)
    factor = np.where(freq == 0, np.sqrt(1.0 / EDGE), np.sqrt(2.0 / EDGE))
    table = (factor * np.cos(np.pi * (2.0 * place + 1.0) * freq / (2.0 * EDGE))).astype(np.float32)

    def halves(m):
        hi = m.astype(ml_dtypes.bfloat16)
        lo = (m - hi.astype(np.float32)).astype(ml_dtypes.bfloat16)
        return hi, lo

    both = np.zeros((2 * EDGE, 2 * EDGE), np.float32)
    both[:EDGE, :EDGE] = table
    both[EDGE:, EDGE:] = table
    split = np.concatenate([table[0::2], table[1::2]], axis=0)
    hi, lo = halves(both.T)
    right_fwd = np.concatenate([hi, hi, lo], axis=0)
    hi, lo = halves(both)
    right_inv = np.concatenate([hi, lo, hi], axis=0)
    hi, lo = halves(split)
    left_fwd = np.concatenate([hi, hi, lo], axis=1)
    hi, lo = halves(split.T)
    left_inv = np.concatenate([hi, hi, lo], axis=1)
    return right_fwd, right_inv, left_fwd, left_inv


def dot(a, b):
    return jnp.dot(a, b, preferred_element_type=F32)


def parts_of(v):
    hi = v.astype(BF16)
    lo = (v - hi.astype(F32)).astype(BF16)
    return hi, lo


def kernel(
    a_hbm, u_hbm, mom_hbm, w_hbm, ids_hbm, cnt_hbm, rf_hbm, ri_hbm, lf_hbm, li_hbm,
    out_ref,
    a_vm, u_vm, mom_vm, w_vm, rf_vm, ri_vm, lf_vm, li_vm,
    ids_ref, cnt_ref, part, y_slots, x_slots, r1, r2, x1_slots, y2_slots,
    code, codes, spread_w, listed, stage,
    load_sem, in_sem,
    y_send, y_recv, x_send, x_recv, x1_send, x1_recv, y2_send, y2_recv,
    c_send, c_recv, g_send, g_recv,
):
    rep = lax.axis_index("rep")
    pos = lax.axis_index("fsdp")
    y = pos // NX
    x = pos % NX

    def at_y(off):
        return ((y + off) % NY) * NX + x

    def at_x(off):
        return y * NX + (x + NX + off) % NX

    def at_rep(off):
        return (rep + off) % NREP

    barrier = pltpu.get_barrier_semaphore()
    for off in range(1, NY):
        pl.semaphore_signal(barrier, inc=1, device_id=(rep, at_y(off)), device_id_type=MESH)
    for off in range(1, NX):
        pl.semaphore_signal(barrier, inc=1, device_id=(rep, at_x(off)), device_id_type=MESH)

    def load(j):
        t = (y + ORDER[j]) % NY
        cols = pl.ds(pl.multiple_of(t * GROUP, GROUP), GROUP)
        return pltpu.make_async_copy(a_hbm.at[:, cols], a_vm.at[j], load_sem.at[j])

    u_copy = pltpu.make_async_copy(u_hbm, u_vm, in_sem.at[0])
    others = [
        pltpu.make_async_copy(src, dst, in_sem.at[n + 1])
        for n, (src, dst) in enumerate(
            [(ids_hbm, ids_ref), (cnt_hbm, cnt_ref), (mom_hbm, mom_vm), (w_hbm, w_vm), (rf_hbm, rf_vm), (ri_hbm, ri_vm), (lf_hbm, lf_vm), (li_hbm, li_vm)]
        )
    ]
    for copy in others[0:2]:
        copy.start()
    u_copy.start()
    for j in range(2):
        load(j).start()

    for off in range(1, NREP):
        pl.semaphore_signal(barrier, inc=1, device_id=(at_rep(off), pos), device_id_type=MESH)

    for j in range(2, NY):
        load(j).start()
    for copy in others[2:]:
        copy.start()

    started = []

    class Sent:
        def __init__(self, src, dst, send, recv, device):
            self.copy = pltpu.make_async_remote_copy(
                src_ref=src, dst_ref=dst, send_sem=send, recv_sem=recv, device_id=device, device_id_type=MESH
            )

        def start(self):
            self.copy.start()
            started.append(self.copy)

        def wait_recv(self):
            self.copy.wait_recv()

    remote = Sent

    y_moves = ((3, 0, NX, 1), (5, 0, NX, -1), (4, 0, 2, 2), (4, 2, 2, -2), (2, 0, NX, 2), (6, 0, NX, -2), (1, 0, NX, 1), (7, 0, NX, -1))

    def y_slot(n):
        return y_slots.at[n, pl.ds(0, y_moves[n][2])]

    def y_copy(n):
        off, first, count, hops = y_moves[n]
        if n == 4 or n == 5:
            src = y_slot(n - 4)
        else:
            src = part.at[ORDER.index(off), pl.ds(first, count), pl.ds(0, H1)]
        return remote(src, y_slot(n), y_send.at[n], y_recv.at[n], (rep, at_y(hops)))

    def y_mid(side):
        first = y_moves[2 + side][1]
        y_copy(side).wait_recv()
        y_copy(2 + side).wait_recv()
        mine = part.at[ORDER.index(y_moves[4 + side][0])]
        near = slice(first, first + 2)
        rest = slice(2 - first, 4 - first)
        total = y_slots[side, near].astype(F32) + y_slots[2 + side, 0:2].astype(F32) + mine[near, 0:H1].astype(F32)
        y_slots[side, near] = total.astype(BF16)
        total = y_slots[side, rest].astype(F32) + mine[rest, 0:H1].astype(F32)
        y_slots[side, rest] = total.astype(BF16)
        y_copy(4 + side).start()

    def x_way(q):
        return 1 - 2 * ((q + rep) % 2)

    def x_copy(q, which):
        way = x_way(q)
        n = 3 * q + which
        rows = pl.ds(2 * q, 2)
        if which == 0:
            src = part.at[rows, (x + 2) % NX, pl.ds(H1, H2)]
        elif which == 1:
            src = x_slots.at[3 * q]
        else:
            src = part.at[rows, (x + NX - way) % NX, pl.ds(H1, H2)]
            way = -way
        return remote(src, x_slots.at[n], x_send.at[n], x_recv.at[n], (rep, at_x(way)))

    def x_mid(q):
        x_copy(q, 0).wait_recv()
        mine = part[2 * q : 2 * q + 2, (x + NX + x_way(q)) % NX, H1:ROWS]
        x_slots[3 * q] = (x_slots[3 * q].astype(F32) + mine.astype(F32)).astype(BF16)
        x_copy(q, 1).start()

    def y2_copy(off):
        j = ORDER.index(off)
        return remote(r2.at[j], y2_slots.at[off - 1], y2_send.at[off - 1], y2_recv.at[off - 1], (rep, at_y(off)))

    def x_last(q):
        x_copy(q, 2).wait_recv()
        x_copy(q, 1).wait_recv()
        mine = part[2 * q : 2 * q + 2, x, H1:ROWS].astype(F32)
        total = mine + x_slots[3 * q + 1].astype(F32) + x_slots[3 * q + 2].astype(F32)
        r2[2 * q : 2 * q + 2] = total.astype(BF16)
        for off in ORDER[2 * q : 2 * q + 2]:
            if off:
                y2_copy(off).start()

    def x1_copy(off):
        return remote(
            r1.at[(x + off) % NX], x1_slots.at[off - 1], x1_send.at[off - 1], x1_recv.at[off - 1], (rep, at_x(off))
        )

    def c_copy(off):
        return remote(code, codes.at[rep], c_send.at[off - 1], c_recv.at[off - 1], (at_rep(off), pos))

    def g_copy(piece, off):
        n = piece * (NREP - 1) + off - 1
        mine = listed.at[PIECES[piece], rep]
        return remote(mine, mine, g_send.at[n], g_recv.at[n], (at_rep(off), pos))

    u_copy.wait()
    grads = u_vm[...].T

    for q in range(STREAMS):
        load(2 * q).wait()
        load(2 * q + 1).wait()
        for j in range(2 * q, 2 * q + 2):
            columns = jnp.dot(grads, a_vm[j], preferred_element_type=F32).astype(BF16)
            part[j] = columns.T.reshape(NX, ROWS, FW)
        if q == 0:
            pl.semaphore_wait(barrier, NY - 1 + NX - 1 + NREP - 1)
            y_copy(0).start()
            y_copy(2).start()
            y_copy(3).start()
        if q == 1:
            y_copy(1).start()
        if q == 2:
            y_copy(6).start()
        if q == 3:
            y_copy(7).start()
        x_copy(q, 0).start()
        if q < 3:
            x_copy(q, 2).start()

    for copy in others[0:2]:
        copy.wait()
    lane8 = lax.broadcasted_iota(jnp.int32, (8, 128), 1)
    row8 = lax.broadcasted_iota(jnp.int32, (8, 128), 0)
    own = lane8 - (rep % 8) * 16
    target = [
        [jnp.where(k < cnt_ref[0, t], ids_ref[t, 0, k], -64) for k in range(SLOTS)] for t in range(2 * TILE_ROWS)
    ]
    codes_own = jnp.where((own >= 0) & (own < 16), -64, 0)
    for k in range(SLOTS):
        column = jnp.zeros((8, 128), jnp.int32)
        for t in range(2 * TILE_ROWS):
            column = jnp.where(row8 == t, target[t][k], column)
        codes_own = jnp.where(own == k, column, codes_own)
        codes_own = jnp.where(own == k + SLOTS, column + NBLK, codes_own)
    code[...] = codes_own
    codes[rep] = codes_own
    stage[...] = jnp.zeros_like(stage)

    y_mid(0)
    x_mid(0)
    y_mid(1)
    x_mid(1)
    x_copy(3, 2).start()
    x_mid(2)
    x_mid(3)
    x_last(0)
    x_last(1)

    total = part[ORDER.index(0), :, 0:H1].astype(F32)
    for n in (6, 7, 4, 5):
        y_copy(n).wait_recv()
        total += y_slots[n].astype(F32)
    r1[...] = total.astype(BF16)
    for off in range(1, NX):
        x1_copy(off).start()
    x_last(2)
    x_last(3)
    for off in range(1, NREP):
        c_copy(off).start()

    for copy in others[2:]:
        copy.wait()

    row64 = lax.broadcasted_iota(jnp.int32, (EDGE, 128), 0)
    lane64 = lax.broadcasted_iota(jnp.int32, (EDGE, 128), 1)
    low_lanes = lane64 < EDGE
    block64 = row64 % NBLK

    def left(table, v):
        out = []
        for a in range(v.shape[0] // EDGE):
            hi, lo = parts_of(v[a * EDGE : a * EDGE + EDGE])
            out.append(dot(table, jnp.concatenate([hi, lo, hi], axis=0)))
        return jnp.concatenate(out, axis=0)

    keep = []

    def list_and_send(piece, moment):
        hi, lo = parts_of(moment)
        coeffs = left(lf_vm[...], dot(jnp.concatenate([hi, lo, hi], axis=1), rf_vm[...])).astype(BF16).astype(F32)
        first = PIECES[piece].start
        for a in range(first, PIECES[piece].stop):
            tile = coeffs[(a - first) * EDGE : (a - first) * EDGE + EDGE]
            live = jnp.zeros((EDGE, 128), F32)
            for k in range(SLOTS):
                chosen = jnp.where(low_lanes, target[2 * a][k], target[2 * a + 1][k]) == block64
                live = jnp.where(chosen, 1.0, live)
                rows = jnp.where(chosen, tile, 0.0)
                stage[a, k : k + 1] = jnp.sum(rows[0:NBLK], axis=0, keepdims=True)
                stage[a, SLOTS + k : SLOTS + k + 1] = jnp.sum(rows[NBLK:EDGE], axis=0, keepdims=True)
            keep.append(tile * live)
            listed[a, rep] = stage[a].astype(BF16)
        for off in REPLICAS:
            g_copy(piece, off).start()

    g1 = r1[x].astype(F32)
    for off in range(1, NX):
        x1_copy(off).wait_recv()
        g1 += x1_slots[off - 1].astype(F32)
    moment1 = 0.9 * mom_vm[0, 0:H1] + g1
    list_and_send(0, moment1)
    g2 = r2[ORDER.index(0)].astype(F32)
    for off in range(1, NY):
        y2_copy(off).wait_recv()
        g2 += y2_slots[off - 1].astype(F32)
    moment2 = 0.9 * mom_vm[0, H1:ROWS] + g2
    list_and_send(1, moment2)

    removed = jnp.concatenate(keep, axis=0).astype(BF16)
    right_inv = ri_vm[...]
    taken = left(li_vm[...], dot(jnp.concatenate([removed, removed], axis=1), right_inv[0:256]))
    out_ref[1, 0:H1] = moment1 - taken[0:H1]
    out_ref[1, H1:ROWS] = moment2 - taken[H1:ROWS]

    for off in range(1, NREP):
        c_copy(off).wait_recv()
    for side in range(NREP // 8):
        tile = codes[8 * side]
        for r in range(1, 8):
            tile += codes[8 * side + r]
        for t in range(2 * TILE_ROWS):
            hit = (tile[t : t + 1] == row64).astype(F32).astype(BF16)
            spread_w[t // 2, EDGE * (t % 2) : EDGE * (t % 2) + EDGE, 128 * side : 128 * side + 128] = hit

    for copy in started:
        copy.wait_send()
    lane1 = lax.broadcasted_iota(jnp.int32, (1, 128), 1) < EDGE
    for piece in range(len(PIECES)):
        for off in range(1, NREP):
            g_copy(piece, off).wait_recv()
        first = PIECES[piece].start
        summed = []
        for a in range(first, PIECES[piece].stop):
            rows = dot(spread_w[a], listed[a].reshape(NREP * 16, 128))
            summed.append(jnp.where(low_lanes, rows[0:EDGE], rows[EDGE : 2 * EDGE]))
        hi, lo = parts_of(jnp.concatenate(summed, axis=0))
        update = left(li_vm[...], dot(jnp.concatenate([hi, hi, lo], axis=1), right_inv))
        for a in range(first, PIECES[piece].stop):
            tile = update[(a - first) * EDGE : (a - first) * EDGE + EDGE]
            squares = jnp.sum(tile * tile, axis=0, keepdims=True)
            low = jnp.sum(jnp.where(lane1, squares, 0.0), axis=1, keepdims=True)
            high = jnp.sum(jnp.where(lane1, 0.0, squares), axis=1, keepdims=True)
            scale = lax.rsqrt(jnp.where(lane1, low, high) * (1.0 / (EDGE * EDGE)) + 1e-6)
            span = slice(a * EDGE, a * EDGE + EDGE)
            out_ref[0, span] = w_vm[span] - 0.25 * jnp.tanh(tile * scale)


def on_device(activations, unit_grads, momentum, weights, block_ids, block_counts):
    right_fwd, right_inv, left_fwd, left_inv = tables()
    hbm = pl.BlockSpec(memory_space=pltpu.HBM)
    dma = pltpu.SemaphoreType.DMA
    both = pl.pallas_call(
        kernel,
        out_shape=pltpu.VMEM((2, ROWS, FW), F32),
        in_specs=[hbm] * 10,
        out_specs=pl.BlockSpec(memory_space=pltpu.VMEM),
        scratch_shapes=[
            pltpu.VMEM((NY, TOK, GROUP), BF16),
            pltpu.VMEM((TOK, FW), BF16),
            pltpu.VMEM((1, ROWS, FW), F32),
            pltpu.VMEM((ROWS, FW), F32),
            pltpu.VMEM(right_fwd.shape, BF16),
            pltpu.VMEM(right_inv.shape, BF16),
            pltpu.VMEM(left_fwd.shape, BF16),
            pltpu.VMEM(left_inv.shape, BF16),
            pltpu.SMEM((2 * TILE_ROWS, 1, SLOTS), jnp.int32),
            pltpu.SMEM((1, 2 * TILE_ROWS), jnp.int32),
            pltpu.VMEM((NY, NX, ROWS, FW), BF16),
            pltpu.VMEM((8, NX, H1, FW), BF16),
            pltpu.VMEM((3 * STREAMS, 2, H2, FW), BF16),
            pltpu.VMEM((NX, H1, FW), BF16),
            pltpu.VMEM((NY, H2, FW), BF16),
            pltpu.VMEM((NX - 1, H1, FW), BF16),
            pltpu.VMEM((NY - 1, H2, FW), BF16),
            pltpu.VMEM((8, 128), jnp.int32),
            pltpu.VMEM((NREP, 8, 128), jnp.int32),
            pltpu.VMEM((TILE_ROWS, 2 * EDGE, NREP * 16), BF16),
            pltpu.VMEM((TILE_ROWS, NREP, 16, 128), BF16),
            pltpu.VMEM((TILE_ROWS, 16, 128), F32),
            dma((NY,)),
            dma((9,)),
            dma((8,)), dma((8,)),
            dma((3 * STREAMS,)), dma((3 * STREAMS,)),
            dma((NX - 1,)), dma((NX - 1,)),
            dma((NY - 1,)), dma((NY - 1,)),
            dma((NREP - 1,)), dma((NREP - 1,)),
            dma((len(PIECES) * (NREP - 1),)), dma((len(PIECES) * (NREP - 1),)),
        ],
        compiler_params=pltpu.CompilerParams(
            collective_id=0, has_side_effects=True, vmem_limit_bytes=60 * 1024 * 1024
        ),
    )(activations, unit_grads, momentum, weights, jnp.transpose(block_ids, (1, 0, 2)), block_counts, right_fwd, right_inv, left_fwd, left_inv)
    return both[0], both[1:2]


def solution(mesh):
    placed = (
        P(("rep", "fsdp"), None),
        P(("rep", "fsdp"), None),
        P("rep", "fsdp", None),
        P("fsdp", None),
        P("rep", "fsdp", None),
        P("rep", "fsdp"),
    )
    return jax.shard_map(
        on_device,
        mesh=mesh,
        in_specs=placed,
        out_specs=(P("fsdp", None), P("rep", "fsdp", None)),
        check_vma=False,
    )
```
